256 devices in a mesh: row: 16 (over x, y_lo, core), col: 16 (over y_hi, z).
Axes of the slice: x: 4, y: 4 (y_hi: 2, y_lo: 2; y = y_hi * 2 + y_lo), z: 8, core: 2. Of those that a mesh axis runs over, the one named last changes fastest.
Arguments:
- points: bfloat16 [24576, 256], P(('row', 'col')), may hold values from -5 to 5
- mass: float32 [24576], P(('row', 'col')), may hold values from 0.05 to 20
Outputs:
- potential: float32 [24576], P(('row', 'col'))
The draws below stay inside these ranges and needn't reach their ends.
All inputs are finite; a program needn't handle non-finite values.
Results may differ from the reference program's by a relative error of at most 0.0003.
Values may be sent and summed in bfloat16 or wider, within the bound.
No kernel may reach another device: no remote copies, remote signals or barrier semaphores. Data moves between devices by JAX's collectives and lax.ppermute only.
A program may use at most 64 MiB of HBM per device.

```python
import math
import jax
import jax.numpy as jnp
from jax import lax

DW = 256
SWEEPS = 3
NPTS = 24576
N_ROW = 16


def cluster_draw(key):
    member_key = jax.random.fold_in(key, 101)
    level_key = jax.random.fold_in(key, 102)
    cluster_ids = jax.random.randint(member_key, (NPTS,), 0, 6)
    levels = jnp.exp(jax.random.uniform(level_key, (6,), jnp.float32, math.log(0.1), math.log(10.0)))
    return (cluster_ids, levels)


def draw_points(key, part):
    cluster_ids = cluster_draw(key)[0]
    key = jax.random.fold_in(key, 7)
    first_key = jax.random.fold_in(key, 0)
    third_key = jax.random.fold_in(key, 2)
    fourth_key = jax.random.fold_in(key, 3)
    fifth_key = jax.random.fold_in(key, 4)
    centres = jax.random.truncated_normal(fourth_key, -3.0, 3.0, (6, DW), jnp.float32) * 0.035
    base_points = jax.random.truncated_normal(first_key, -5.0, 5.0, (NPTS, DW), jnp.float32) / 16.0
    placed = centres[cluster_ids] + base_points
    copies = jax.random.randint(fifth_key, (NPTS, 1), 0, 16) == 0
    offset = NPTS // 2 + 1
    scaled = placed
    noise = jax.random.truncated_normal(third_key, -4.0, 4.0, (NPTS, DW), jnp.float32) * 0.02
    partner = jnp.roll(scaled, offset, axis=0)
    result = jnp.where(copies, partner + noise, scaled)
    return result.astype(jnp.bfloat16)


def draw_mass(key, part):
    cluster_ids, levels = cluster_draw(key)
    key = jax.random.fold_in(key, 11)
    factor = jnp.exp(jax.random.uniform(key, (NPTS,), jnp.float32, math.log(0.5), math.log(2.0)))
    return levels[cluster_ids] * factor


def setup_inputs(seed: int = 0) -> dict:
    streams_of = jax.random.split(jax.random.key(seed), 3)
    points = draw_points(jax.random.fold_in(streams_of[2], 71), 0)
    mass = draw_mass(jax.random.fold_in(streams_of[2], 71), 0)
    return {"points": points, "mass": mass}


epsilon_value = 0.1


def reference(points, mass):
    squares = jnp.sum(jnp.square(points.astype(jnp.float32)), axis=1)
    log_weight = jnp.log(mass) - math.log(NPTS)
    block_rows = NPTS // N_ROW
    row_blocks = points.reshape(N_ROW, block_rows, DW)
    potential = jnp.zeros((NPTS,), jnp.float32)
    for sweep_index in range(SWEEPS):
        log_terms = log_weight + potential / epsilon_value - 0.5 * squares / epsilon_value

        def block_lse(row_points):
            scores = log_terms[None, :] + jnp.dot(row_points, points.T, preferred_element_type=jnp.float32) / epsilon_value
            largest = jnp.max(scores, axis=1)
            return largest + jnp.log(jnp.sum(jnp.exp(scores - largest[:, None]), axis=1))

        log_sums = lax.map(block_lse, row_blocks).reshape(NPTS)
        potential = 0.5 * (potential + (0.5 * squares - epsilon_value * log_sums))
    return potential / epsilon_value
```

```python
import jax
import jax.numpy as jnp
from jax import lax
from jax.sharding import Mesh
from jax.sharding import PartitionSpec as P

SWEEPS = 3
EPSILON = 0.1
AXES = ("x", "yl", "k", "yh", "z")
ROW = ("x", "yl", "k")
COL = ("yh", "z")


def copies(array, count):
    return jnp.broadcast_to(array[None], (count,) + array.shape)


def gathered(array, axes, count):
    return lax.all_to_all(copies(array, count), axes, 0, 0)


def mass_parts(mass):
    high = lax.reduce_precision(mass, 8, 7)
    middle = lax.reduce_precision(mass - high, 8, 7)
    low = mass - high - middle
    return jnp.stack([high, middle, low]).astype(jnp.bfloat16)


def shards(points, mass):
    own, width = points.shape
    n_row, n_col = 16, 16
    total = own * n_row * n_col
    parts = jnp.pad(mass_parts(mass), ((0, 13), (0, width - own)))
    column = gathered(jnp.concatenate([points, parts], 0), COL, n_col)
    right = column[:, :own].reshape(n_col * own, width)
    right_mass = jnp.sum(column[:, own : own + 3, :own].astype(jnp.float32), axis=1).reshape(n_col * own)
    left = gathered(points, ("x", "yl"), 8)
    left = lax.all_gather(left, "k", axis=1).reshape(n_row * own, width)
    right_squares = jnp.sum(jnp.square(right.astype(jnp.float32)), axis=1)
    left_squares = jnp.sum(jnp.square(left.astype(jnp.float32)), axis=1)
    inner = lax.dot_general(right, left, (((1,), (1,)), ((), ())), preferred_element_type=jnp.float32)
    kernel = jnp.exp((inner - 0.5 * right_squares[:, None] - 0.5 * left_squares[None, :]) / EPSILON)
    sums = jnp.sum(kernel * (right_mass / total)[:, None], axis=0)
    got = gathered(jnp.concatenate([sums, mass]), ROW, n_row)
    left_f = -0.5 * jnp.log(jnp.sum(got[:, : n_row * own], axis=0))
    left_mass = got[:, n_row * own :].reshape(n_row * own)
    left_weight = (left_mass / total) * jnp.exp(left_f)
    sums = jnp.sum(kernel * left_weight[None, :], axis=1)
    row = lax.axis_index(ROW)
    own_f = lax.dynamic_slice_in_dim(left_f, row * own, own)
    got = gathered(jnp.concatenate([sums, own_f]), COL, n_col)
    right_f = got[:, n_col * own :].reshape(n_col * own)
    right_f = 0.5 * (right_f - jnp.log(jnp.sum(got[:, : n_col * own], axis=0)))
    right_weight = (right_mass / total) * jnp.exp(right_f)
    sums = jnp.sum(kernel * right_weight[:, None], axis=0).reshape(n_row, 1, own)
    sums = jnp.sum(lax.all_to_all(sums, ROW, 0, 0), axis=(0, 1))
    col = lax.axis_index(COL)
    own_f = lax.dynamic_slice_in_dim(right_f, col * own, own)
    return 0.5 * (own_f - jnp.log(sums))


def solution(mesh):
    fine = Mesh(mesh.devices.reshape(4, 2, 2, 2, 8), AXES)
    return jax.shard_map(
        shards,
        mesh=fine,
        in_specs=(P(AXES, None), P(AXES)),
        out_specs=P(AXES),
        check_vma=False,
    )
```

```python
import functools
import math

import jax
import jax.numpy as jnp
from jax import lax
from jax.experimental import pallas as pl
from jax.experimental.pallas import tpu as pltpu
from jax.sharding import Mesh
from jax.sharding import PartitionSpec as P

EPSILON = 0.1
AXES = ("x", "yl", "k", "yh", "z")
ROW = ("x", "yl", "k")
COL = ("yh", "z")
LANES = 128
STEP = 256
SCALE = math.log2(math.e) / EPSILON
VMEM = pl.BlockSpec(memory_space=pltpu.VMEM)
SMEM = pl.BlockSpec(memory_space=pltpu.SMEM)
PARAMS = pltpu.CompilerParams(vmem_limit_bytes=40 * 2**20)


def lane_pieces(length):
    return [slice(n, n + LANES) for n in range(0, length, LANES)]


def store_columns(row, columns_ref):
    for piece in lane_pieces(row.shape[1]):
        columns_ref[piece, :] = jnp.broadcast_to(row[:, piece], (LANES, LANES)).T


def repeated(column, length):
    return jnp.concatenate([column] * (length // LANES), axis=1)


def row_of_sums(partial_ref):
    return jnp.concatenate(
        [jnp.sum(partial_ref[piece, :].T, axis=0, keepdims=True) for piece in lane_pieces(partial_ref.shape[0])],
        axis=1,
    )


def copies_kernel(points_ref, mass_ref, send_ref):
    own, width = points_ref.shape
    mass = mass_ref[...]
    high = mass.astype(jnp.bfloat16).astype(jnp.float32)
    middle = (mass - high).astype(jnp.bfloat16).astype(jnp.float32)
    low = mass - high - middle
    parts = jnp.concatenate([high, middle, low, jnp.zeros((5, own), jnp.float32)], axis=0)
    parts = jnp.concatenate([parts, jnp.zeros((8, width - own), jnp.float32)], axis=1)
    block = jnp.concatenate([points_ref[...].astype(jnp.float32), parts], axis=0).astype(jnp.bfloat16)
    for d in range(send_ref.shape[0]):
        send_ref[d] = block


def left_kernel(rank_ref, near_ref, far_ref, left_ref, squares_ref, partial):
    rank = rank_ref[0]
    for core, ref in enumerate((near_ref, far_ref)):
        for y in range(2):
            for x in range(4):
                place = rank ^ (4 * x + 2 * y + core)
                block = ref[2 * x + y]
                left_ref[place] = block
                wide = block.astype(jnp.float32)
                partial[place] = wide[:, :LANES] * wide[:, :LANES] + wide[:, LANES:] * wide[:, LANES:]
    flat = partial.reshape(partial.shape[0] * partial.shape[1], LANES)
    squares_ref[...] = (-0.5 * SCALE) * row_of_sums(flat)


def concatenated(ref, start, size):
    return jnp.concatenate([ref[d, :, start : start + size] for d in range(ref.shape[0])], axis=1)


def build_kernel(total, column_ref, left_ref, squares_ref, mass_ref, kernel_ref, send_ref, weight_ref, right, columns):
    groups, own = left_ref.shape[0], left_ref.shape[1]
    length = groups * own
    masses = []
    for d in range(groups):
        right[d * own : (d + 1) * own, :] = column_ref[d, :own, :]
        parts = column_ref[d].astype(jnp.float32)[own : own + 3, :own]
        masses.append(jnp.sum(parts, axis=0, keepdims=True))
    weight = jnp.concatenate(masses, axis=1) * (1.0 / total)
    weight_ref[...] = weight
    store_columns(weight, columns)
    left = left_ref[...].reshape(length, left_ref.shape[2])
    left_squares = squares_ref[...]

    def step(n, sums):
        rows = pl.ds(pl.multiple_of(n * STEP, STEP), STEP)
        block = right[rows, :]
        wide = block.astype(jnp.float32)
        right_squares = (-0.5 * SCALE) * jnp.sum(wide * wide, axis=1, keepdims=True)
        inner = lax.dot_general(block, left, (((1,), (1,)), ((), ())), preferred_element_type=jnp.float32)
        entries = jnp.exp2(SCALE * inner + right_squares + left_squares)
        kernel_ref[rows, :] = entries
        weighted = entries * repeated(columns[rows, :], length)
        return sums + jnp.sum(weighted.reshape(STEP // 8, 8, length), axis=0)

    sums = lax.fori_loop(0, length // STEP, step, jnp.zeros((8, length), jnp.float32))
    sums = jnp.sum(sums, axis=0, keepdims=True)
    send = jnp.concatenate([sums, mass_ref[...], jnp.zeros((1, LANES - own), jnp.float32)], axis=1)
    for d in range(groups):
        send_ref[d] = send


def row_sums_kernel(total, own, rank_ref, kernel_ref, got_ref, send_ref, partial):
    groups = got_ref.shape[0]
    length = groups * own
    sums = jnp.sum(got_ref[:, :, :length], axis=0)
    potential = -0.5 * jnp.log(sums)
    mass = concatenated(got_ref, length, own)
    weight = (mass * (1.0 / total)) * jnp.exp(potential)

    def step(n, carry):
        rows = pl.ds(pl.multiple_of(n * 64, 64), 64)
        weighted = kernel_ref[rows, :] * weight
        partial[rows, :] = sum(weighted[:, piece] for piece in lane_pieces(length))
        return carry

    lax.fori_loop(0, length // 64, step, 0)
    mine = jnp.zeros((1, own), jnp.float32)
    for d in range(groups):
        mine = mine + jnp.where(rank_ref[0] == d, potential[:, d * own : (d + 1) * own], 0.0)
    pad = jnp.zeros((1, LANES - own), jnp.float32)
    send = jnp.concatenate([row_of_sums(partial), mine, pad], axis=1)
    for d in range(groups):
        send_ref[d] = send


def column_sums_kernel(own, rank_ref, kernel_ref, got_ref, weight_ref, send_ref, mine_ref, columns):
    groups = got_ref.shape[0]
    length = groups * own
    sums = jnp.sum(got_ref[:, :, :length], axis=0)
    potential = 0.5 * (concatenated(got_ref, length, own) - jnp.log(sums))
    store_columns(weight_ref[...] * jnp.exp(potential), columns)

    def step(n, sums):
        rows = pl.ds(pl.multiple_of(n * 64, 64), 64)
        weighted = kernel_ref[rows, :] * repeated(columns[rows, :], length)
        return sums + jnp.sum(weighted.reshape(8, 8, length), axis=0)

    sums = lax.fori_loop(0, length // 64, step, jnp.zeros((8, length), jnp.float32))
    sums = jnp.sum(sums, axis=0, keepdims=True)
    mine = jnp.zeros((1, own), jnp.float32)
    for d in range(groups):
        mine = mine + jnp.where(rank_ref[1] == d, potential[:, d * own : (d + 1) * own], 0.0)
        send_ref[d, :, :own] = sums[:, d * own : (d + 1) * own]
    mine_ref[...] = mine


def shards(points, mass):
    own, width = points.shape
    groups = 16
    length = groups * own
    total = length * groups
    f32 = jnp.float32
    ranks = jnp.stack([lax.axis_index(ROW), lax.axis_index(COL)]).astype(jnp.int32)
    mass = mass.reshape(1, own)
    send = pl.pallas_call(
        copies_kernel,
        out_shape=jax.ShapeDtypeStruct((groups, own + 8, width), points.dtype),
        in_specs=[VMEM, VMEM],
        out_specs=VMEM,
        compiler_params=PARAMS,
    )(points, mass)
    column = lax.all_to_all(send, COL, 0, 0)
    swap = lambda size, by: [(i, i ^ by) for i in range(size)]
    near = jnp.stack([points, lax.ppermute(points, "yl", swap(2, 1))])
    near = jnp.concatenate([near] + [lax.ppermute(near, "x", swap(4, s)) for s in (1, 2, 3)])
    far = lax.ppermute(near, "k", swap(2, 1))
    left, left_squares = pl.pallas_call(
        left_kernel,
        out_shape=[jax.ShapeDtypeStruct((groups, own, width), points.dtype), jax.ShapeDtypeStruct((1, length), f32)],
        in_specs=[SMEM, VMEM, VMEM],
        out_specs=[VMEM, VMEM],
        scratch_shapes=[pltpu.VMEM((groups, own, LANES), f32)],
        compiler_params=PARAMS,
    )(ranks, near, far)
    message = jax.ShapeDtypeStruct((groups, 1, length + LANES), f32)
    kernel, send, weight = pl.pallas_call(
        functools.partial(build_kernel, total),
        out_shape=[jax.ShapeDtypeStruct((length, length), f32), message, jax.ShapeDtypeStruct((1, length), f32)],
        in_specs=[VMEM] * 4,
        out_specs=[VMEM] * 3,
        scratch_shapes=[pltpu.VMEM((length, width), points.dtype), pltpu.VMEM((length, LANES), f32)],
        compiler_params=PARAMS,
    )(column, left, left_squares, mass)
    got = lax.all_to_all(send, ROW, 0, 0)
    send = pl.pallas_call(
        functools.partial(row_sums_kernel, total, own),
        out_shape=message,
        in_specs=[SMEM, VMEM, VMEM],
        out_specs=VMEM,
        scratch_shapes=[pltpu.VMEM((length, LANES), f32)],
        compiler_params=PARAMS,
    )(ranks, kernel, got)
    got = lax.all_to_all(send, COL, 0, 0)
    send, mine = pl.pallas_call(
        functools.partial(column_sums_kernel, own),
        out_shape=[jax.ShapeDtypeStruct((groups, 1, own), f32), jax.ShapeDtypeStruct((1, own), f32)],
        in_specs=[SMEM, VMEM, VMEM, VMEM],
        out_specs=[VMEM, VMEM],
        scratch_shapes=[pltpu.VMEM((length, LANES), f32)],
        compiler_params=PARAMS,
    )(ranks, kernel, got, weight)
    sums = jnp.sum(lax.all_to_all(send, ROW, 0, 0), axis=0)
    return (0.5 * (mine - jnp.log(sums))).reshape(own)


def solution(mesh):
    fine = Mesh(mesh.devices.reshape(4, 2, 2, 2, 8), AXES)
    return jax.shard_map(
        shards,
        mesh=fine,
        in_specs=(P(AXES, None), P(AXES)),
        out_specs=P(AXES),
        check_vma=False,
    )
```

```python
import functools
import math

import jax
import jax.numpy as jnp
from jax import lax
from jax.experimental import pallas as pl
from jax.experimental.pallas import tpu as pltpu
from jax.sharding import Mesh
from jax.sharding import PartitionSpec as P

EPSILON = 0.1
AXES = ("x", "yl", "k", "yh", "z")
ROW = ("x", "yl", "yh")
COL = ("k", "z")
DELTAS = (0, 1, -1, 4, 2, 3, -2, -3)
LANES = 128
TILE = 256
ROWS = 384
EXTRA = 8
LOG2E = math.log2(math.e)
SCALE = LOG2E / EPSILON
VMEM = pl.BlockSpec(memory_space=pltpu.VMEM)
HBM = pl.BlockSpec(memory_space=pltpu.HBM)
SMEM = pl.BlockSpec(memory_space=pltpu.SMEM)
PARAMS = pltpu.CompilerParams(vmem_limit_bytes=40 * 2**20)


def lane_pieces(length):
    return [slice(n, n + LANES) for n in range(0, length, LANES)]


def store_columns(pieces, columns_ref):
    for n, piece in enumerate(pieces):
        columns_ref[n * LANES : (n + 1) * LANES, :] = jnp.broadcast_to(piece, (LANES, LANES)).T


def repeated(column, length):
    return jnp.concatenate([column] * (length // LANES), axis=1)


def row_of_sums(partial):
    return jnp.sum(partial.T, axis=0, keepdims=True)


def from_z(array, delta):
    return lax.ppermute(array, "z", [(z, (z - delta) % 8) for z in range(8)])


def three_parts(row):
    high = row.astype(jnp.bfloat16).astype(jnp.float32)
    middle = (row - high).astype(jnp.bfloat16).astype(jnp.float32)
    return [high, middle, row - high - middle]


def copies_kernel(total, points_ref, mass_ref, send_ref, block_ref, held, held_mass, read, written):
    own, width = points_ref.shape
    reads = [pltpu.make_async_copy(points_ref, held, read.at[0]), pltpu.make_async_copy(mass_ref, held_mass, read.at[1])]
    for copy in reads:
        copy.start()
    for copy in reads:
        copy.wait()
    copies = [pltpu.make_async_copy(held, send_ref.at[d], written.at[d]) for d in range(send_ref.shape[0])]
    for copy in copies:
        copy.start()
    mass = held_mass[...]
    wide = held[...].astype(jnp.float32)
    halves = [wide[:, :LANES], wide[:, LANES:]]
    squares = halves[0] * halves[0] + halves[1] * halves[1]
    squares = jnp.concatenate([squares, jnp.zeros((LANES - own, LANES), jnp.float32)], axis=0)
    squares = row_of_sums(squares)[:, :own]
    base = LOG2E * jnp.log(mass * (1.0 / total)) - (0.5 * SCALE) * squares
    rows = three_parts(base) + three_parts(mass)
    rows.append(jnp.zeros((EXTRA - len(rows), own), jnp.float32))
    rows = jnp.concatenate(rows, axis=0)
    rows = jnp.concatenate([rows, jnp.zeros((EXTRA, LANES - own), jnp.float32)], axis=1)
    block_ref[...] = jnp.concatenate(halves + [rows], axis=0).astype(jnp.bfloat16)
    for copy in copies:
        copy.wait()


def right_kernel(rank_ref, near_ref, far_ref, right_ref, columns_ref, mass_ref):
    own = right_ref.shape[1]
    rank = rank_ref[1]
    for core, ref in enumerate((near_ref, far_ref)):
        for n, delta in enumerate(DELTAS):
            place = ((rank & 8) ^ (8 * core)) + ((rank + delta) & 7)
            right_ref[place, :, :LANES] = ref[n, :own, :]
            right_ref[place, :, LANES:] = ref[n, own : 2 * own, :]
            extra = ref[n].astype(jnp.float32)[2 * own :]
            base = jnp.sum(extra[0:3], axis=0, keepdims=True)
            columns_ref[place] = jnp.broadcast_to(base, (LANES, LANES)).T[:own]
    extra = near_ref[0].astype(jnp.float32)[2 * own :]
    mass_ref[...] = jnp.sum(extra[3:6], axis=0, keepdims=True)


def build_kernel(right_ref, columns_ref, mass_ref, left_ref, kernel_ref, send_ref):
    groups, own, width = left_ref.shape
    length = groups * own
    right = right_ref.reshape(length, width)
    columns = columns_ref.reshape(length, LANES)
    left = left_ref.reshape(length, width)
    sums = []
    for tile in range(0, length, TILE):
        squares = []
        for piece in range(tile, tile + TILE, LANES):
            wide = left[piece : piece + LANES, :].astype(jnp.float32)
            squares.append(row_of_sums(wide[:, :LANES] * wide[:, :LANES] + wide[:, LANES:] * wide[:, LANES:]))
        left_squares = (-0.5 * SCALE) * jnp.concatenate(squares, axis=1)
        total = jnp.zeros((8, TILE), jnp.float32)
        for start in range(0, length, ROWS):
            rows = slice(start, start + ROWS)
            inner = lax.dot_general(
                right[rows, :], left[tile : tile + TILE, :], (((1,), (1,)), ((), ())), preferred_element_type=jnp.float32
            )
            entries = jnp.exp2((SCALE * inner + left_squares) + repeated(columns[rows, :], TILE))
            kernel_ref[rows, tile : tile + TILE] = entries
            total = total + jnp.sum(entries.reshape(ROWS // 8, 8, TILE), axis=0)
        sums.append(jnp.sum(total, axis=0, keepdims=True))
    pieces = [total[:, piece] for total in sums for piece in lane_pieces(TILE)]
    send = jnp.concatenate(pieces + [mass_ref[...]], axis=1)
    for d in range(groups):
        send_ref[d] = send


def last_rows(got_ref, length, own):
    return jnp.concatenate([got_ref[d, :, length : length + own] for d in range(got_ref.shape[0])], axis=1)


def as_rows(row):
    return jnp.concatenate([row[:, piece] for piece in lane_pieces(row.shape[1])], axis=0)


def own_piece(flat_ref, rank, own):
    start = rank * own
    row, lane = start // LANES, start % LANES
    shift = (LANES - lane) % LANES
    first = pltpu.roll(jnp.broadcast_to(flat_ref[pl.ds(row, 1), :], (8, LANES)), shift, 1)
    second = pltpu.roll(jnp.broadcast_to(flat_ref[pl.ds(row + 1, 1), :], (8, LANES)), shift, 1)
    lanes = lax.broadcasted_iota(jnp.int32, (8, LANES), 1)
    return jnp.where(lanes < LANES - lane, first, second)[0:1]


def row_sums_kernel(total, own, rank_ref, kernel_ref, got_ref, send_ref, partial, flat):
    groups = got_ref.shape[0]
    length = groups * own
    count = length // LANES
    potential = -0.5 * jnp.log(as_rows(jnp.sum(got_ref[:, :, :length], axis=0)))
    flat[:count, :] = potential
    flat[count:, :] = jnp.zeros((flat.shape[0] - count, LANES), jnp.float32)
    growth = jnp.exp(potential)
    mass = last_rows(got_ref, length, own) * (1.0 / total)
    weight = jnp.concatenate([growth[n : n + 1] * mass[:, piece] for n, piece in enumerate(lane_pieces(length))], axis=1)

    def step(n, carry):
        rows = pl.ds(pl.multiple_of(n * 256, 256), 256)
        weighted = kernel_ref[rows, :] * weight
        partial[rows, :] = sum(weighted[:, piece] for piece in lane_pieces(length))
        return carry

    lax.fori_loop(0, length // 256, step, 0)
    own_mass = got_ref[rank_ref[0], :, length:] * (1.0 / total)
    mine = own_piece(flat, rank_ref[0], own) + jnp.log(own_mass)
    pieces = [row_of_sums(partial[piece, :]) for piece in lane_pieces(length)]
    send = jnp.concatenate(pieces + [mine], axis=1)
    for d in range(groups):
        send_ref[d] = send


def column_sums_kernel(own, rank_ref, kernel_ref, got_ref, send_ref, mine_ref, columns, flat):
    groups = got_ref.shape[0]
    length = groups * own
    count = length // LANES
    logs = jnp.log(as_rows(jnp.sum(got_ref[:, :, :length], axis=0)))
    before = as_rows(last_rows(got_ref, length, own))
    potential = 0.5 * (before - logs)
    flat[:count, :] = potential
    flat[count:, :] = jnp.zeros((flat.shape[0] - count, LANES), jnp.float32)
    growth = jnp.exp(potential)
    store_columns([growth[n : n + 1] for n in range(count)], columns)

    def step(n, sums):
        rows = pl.ds(pl.multiple_of(n * 16, 16), 16)
        weighted = kernel_ref[rows, :] * repeated(columns[rows, :], length)
        return sums + (weighted[:8] + weighted[8:])

    sums = lax.fori_loop(0, length // 16, step, jnp.zeros((8, length), jnp.float32), unroll=4)
    sums = jnp.sum(sums, axis=0, keepdims=True)
    for d in range(groups):
        send_ref[d] = sums[:, d * own : (d + 1) * own]
    mine_ref[...] = own_piece(flat, rank_ref[1], own)[:, :own]


def shards(points, mass):
    own, width = points.shape
    groups = 16
    length = groups * own
    total = length * groups
    f32 = jnp.float32
    ranks = jnp.stack([lax.axis_index(ROW), lax.axis_index(COL)]).astype(jnp.int32)
    send, block = pl.pallas_call(
        functools.partial(copies_kernel, total),
        out_shape=[
            jax.ShapeDtypeStruct((groups, own, width), points.dtype),
            jax.ShapeDtypeStruct((2 * own + EXTRA, LANES), points.dtype),
        ],
        in_specs=[HBM, HBM],
        out_specs=[HBM, VMEM],
        scratch_shapes=[
            pltpu.VMEM((own, width), points.dtype),
            pltpu.VMEM((1, own), f32),
            pltpu.SemaphoreType.DMA((2,)),
            pltpu.SemaphoreType.DMA((groups,)),
        ],
        compiler_params=PARAMS,
    )(points, mass.reshape(1, own))
    left = lax.all_to_all(send, ROW, 0, 0)
    above, below, across = from_z(block, 1), from_z(block, -1), from_z(block, 4)
    near = [jnp.stack([block, above, below, across])]
    near += [from_z(jnp.stack([block, above]), 2), from_z(jnp.stack([block, below]), -2)]
    near = jnp.concatenate(near)
    far = lax.ppermute(near, "k", [(0, 1), (1, 0)])
    right, columns, own_mass = pl.pallas_call(
        right_kernel,
        out_shape=[
            jax.ShapeDtypeStruct((groups, own, width), points.dtype),
            jax.ShapeDtypeStruct((groups, own, LANES), f32),
            jax.ShapeDtypeStruct((1, LANES), f32),
        ],
        in_specs=[SMEM, VMEM, VMEM],
        out_specs=[VMEM, VMEM, VMEM],
        compiler_params=PARAMS,
    )(ranks, near, far)
    message = jax.ShapeDtypeStruct((groups, 1, length + LANES), f32)
    kernel, send = pl.pallas_call(
        build_kernel,
        out_shape=[jax.ShapeDtypeStruct((length, length), f32), message],
        in_specs=[VMEM] * 4,
        out_specs=[VMEM, VMEM],
        compiler_params=PARAMS,
    )(right, columns, own_mass, left)
    got = lax.all_to_all(send, ROW, 0, 0)
    send = pl.pallas_call(
        functools.partial(row_sums_kernel, total, own),
        out_shape=message,
        in_specs=[SMEM, VMEM, VMEM],
        out_specs=VMEM,
        scratch_shapes=[pltpu.VMEM((length, LANES), f32), pltpu.VMEM((16, LANES), f32)],
        compiler_params=PARAMS,
    )(ranks, kernel, got)
    got = lax.all_to_all(send, COL, 0, 0)
    send, mine = pl.pallas_call(
        functools.partial(column_sums_kernel, own),
        out_shape=[jax.ShapeDtypeStruct((groups, 1, own), f32), jax.ShapeDtypeStruct((1, own), f32)],
        in_specs=[SMEM, VMEM, VMEM],
        out_specs=[VMEM, VMEM],
        scratch_shapes=[pltpu.VMEM((length, LANES), f32), pltpu.VMEM((16, LANES), f32)],
        compiler_params=PARAMS,
    )(ranks, kernel, got)
    sums = jnp.sum(lax.all_to_all(send, ROW, 0, 0), axis=0)
    return (0.5 * (mine - jnp.log(sums))).reshape(own)


def solution(mesh):
    fine = Mesh(mesh.devices.reshape(4, 2, 2, 2, 8), AXES)
    return jax.shard_map(
        shards,
        mesh=fine,
        in_specs=(P(AXES, None), P(AXES)),
        out_specs=P(AXES),
        check_vma=False,
    )
```

```python
import functools
import math

import jax
import jax.numpy as jnp
from jax import lax
from jax.experimental import pallas as pl
from jax.experimental.pallas import tpu as pltpu
from jax.sharding import Mesh
from jax.sharding import PartitionSpec as P

EPSILON = 0.1
AXES = ("x", "yl", "k", "yh", "z")
ROW = ("x", "yl", "yh")
COL = ("k", "z")
SIDE = ((1, 0), (1, 1), (2, 0), (2, 1), (3, 0), (3, 1), (4, 0))
LANES = 128
TILE = 512
ROWS = 768
EXTRA = 8
LOG2E = math.log2(math.e)
SCALE = LOG2E / EPSILON
VMEM = pl.BlockSpec(memory_space=pltpu.VMEM)
HBM = pl.BlockSpec(memory_space=pltpu.HBM)
SMEM = pl.BlockSpec(memory_space=pltpu.SMEM)
PARAMS = pltpu.CompilerParams(vmem_limit_bytes=40 * 2**20)


def lane_pieces(length):
    return [slice(n, n + LANES) for n in range(0, length, LANES)]


def store_columns(pieces, columns_ref):
    for n, piece in enumerate(pieces):
        columns_ref[n * LANES : (n + 1) * LANES, :] = jnp.broadcast_to(piece, (LANES, LANES)).T


def repeated(column, length):
    return jnp.concatenate([column] * (length // LANES), axis=1)


def row_of_sums(partial):
    return jnp.sum(partial.T, axis=0, keepdims=True)


def along_z(array, step):
    pairs = [(z, (z - step) % 8) for z in range(8)] + [(8 + z, 8 + (z + step) % 8) for z in range(8)]
    return lax.ppermute(array, ("k", "z"), pairs)


def three_parts(row):
    high = row.astype(jnp.bfloat16).astype(jnp.float32)
    middle = (row - high).astype(jnp.bfloat16).astype(jnp.float32)
    return [high, middle, row - high - middle]


def copies_kernel(total, points_ref, mass_ref, send_ref, block_ref, held, held_mass, read, written):
    own, width = points_ref.shape
    reads = [pltpu.make_async_copy(points_ref, held, read.at[0]), pltpu.make_async_copy(mass_ref, held_mass, read.at[1])]
    for copy in reads:
        copy.start()
    for copy in reads:
        copy.wait()
    copies = [pltpu.make_async_copy(held, send_ref.at[d], written.at[d]) for d in range(send_ref.shape[0])]
    for copy in copies:
        copy.start()
    mass = held_mass[...]
    wide = held[...].astype(jnp.float32)
    halves = [wide[:, :LANES], wide[:, LANES:]]
    squares = halves[0] * halves[0] + halves[1] * halves[1]
    squares = jnp.concatenate([squares, jnp.zeros((LANES - own, LANES), jnp.float32)], axis=0)
    squares = row_of_sums(squares)[:, :own]
    base = LOG2E * jnp.log(mass * (1.0 / total)) - (0.5 * SCALE) * squares
    rows = three_parts(base) + three_parts(mass)
    rows.append(jnp.zeros((EXTRA - len(rows), own), jnp.float32))
    rows = jnp.concatenate(rows, axis=0)
    rows = jnp.concatenate([rows, jnp.zeros((EXTRA, LANES - own), jnp.float32)], axis=1)
    block_ref[...] = jnp.concatenate(halves + [rows], axis=0).astype(jnp.bfloat16)
    for copy in copies:
        copy.wait()


def place_blocks(blocks_ref, places, core, z, right_ref, columns_ref):
    own = right_ref.shape[1]
    for n, (distance, other) in enumerate(places):
        place = 8 * (core ^ other) + ((z + (1 - 2 * core) * distance) & 7)
        right_ref[place, :, :LANES] = blocks_ref[n, :own, :]
        right_ref[place, :, LANES:] = blocks_ref[n, own : 2 * own, :]
        extra = blocks_ref[n].astype(jnp.float32)[2 * own :]
        base = jnp.sum(extra[0:3], axis=0, keepdims=True)
        columns_ref[place] = jnp.broadcast_to(base, (LANES, LANES)).T[:own]


def near_kernel(rank_ref, pair_ref, blocks_ref, right_ref, columns_ref, mass_ref):
    core, z = rank_ref[1] // 8, rank_ref[1] % 8
    place_blocks(pair_ref, ((0, 0), (0, 1)), core, z, right_ref, columns_ref)
    place_blocks(blocks_ref, SIDE, core, z, right_ref, columns_ref)
    extra = pair_ref[0].astype(jnp.float32)[2 * right_ref.shape[1] :]
    mass_ref[...] = jnp.sum(extra[3:6], axis=0, keepdims=True)


def far_kernel(rank_ref, blocks_ref, half_right_ref, half_columns_ref, right_ref, columns_ref):
    core, z = rank_ref[1] // 8, rank_ref[1] % 8
    place_blocks(blocks_ref, SIDE, 1 - core, z, right_ref, columns_ref)


def build_kernel(right_ref, columns_ref, mass_ref, left_ref, kernel_ref, send_ref):
    groups, own, width = left_ref.shape
    length = groups * own
    right = right_ref.reshape(length, width)
    columns = columns_ref.reshape(length, LANES)
    left = left_ref.reshape(length, width)
    sums = []
    for tile in range(0, length, TILE):
        squares = []
        for piece in range(tile, tile + TILE, LANES):
            wide = left[piece : piece + LANES, :].astype(jnp.float32)
            squares.append(row_of_sums(wide[:, :LANES] * wide[:, :LANES] + wide[:, LANES:] * wide[:, LANES:]))
        left_squares = (-0.5 * SCALE) * jnp.concatenate(squares, axis=1)
        total = jnp.zeros((8, TILE), jnp.float32)
        for start in range(0, length, ROWS):
            rows = slice(start, start + ROWS)
            inner = lax.dot_general(
                right[rows, :], left[tile : tile + TILE, :], (((1,), (1,)), ((), ())), preferred_element_type=jnp.float32
            )
            entries = jnp.exp2((SCALE * inner + left_squares) + repeated(columns[rows, :], TILE))
            kernel_ref[rows, tile : tile + TILE] = entries
            total = total + jnp.sum(entries.reshape(ROWS // 8, 8, TILE), axis=0)
        sums.append(jnp.sum(total, axis=0, keepdims=True))
    pieces = [total[:, piece] for total in sums for piece in lane_pieces(TILE)]
    send = jnp.concatenate(pieces + [mass_ref[...]], axis=1)
    for d in range(groups):
        send_ref[d] = send


def last_rows(got_ref, length, own):
    return jnp.concatenate([got_ref[d, :, length : length + own] for d in range(got_ref.shape[0])], axis=1)


def as_rows(row):
    return jnp.concatenate([row[:, piece] for piece in lane_pieces(row.shape[1])], axis=0)


def own_piece(flat_ref, rank, own):
    start = rank * own
    row, lane = start // LANES, start % LANES
    shift = (LANES - lane) % LANES
    first = pltpu.roll(jnp.broadcast_to(flat_ref[pl.ds(row, 1), :], (8, LANES)), shift, 1)
    second = pltpu.roll(jnp.broadcast_to(flat_ref[pl.ds(row + 1, 1), :], (8, LANES)), shift, 1)
    lanes = lax.broadcasted_iota(jnp.int32, (8, LANES), 1)
    return jnp.where(lanes < LANES - lane, first, second)[0:1]


def row_sums_kernel(total, own, rank_ref, kernel_ref, got_ref, send_ref, partial, flat):
    groups = got_ref.shape[0]
    length = groups * own
    count = length // LANES
    potential = -0.5 * jnp.log(as_rows(jnp.sum(got_ref[:, :, :length], axis=0)))
    flat[:count, :] = potential
    flat[count:, :] = jnp.zeros((flat.shape[0] - count, LANES), jnp.float32)
    growth = jnp.exp(potential)
    mass = last_rows(got_ref, length, own) * (1.0 / total)
    weight = jnp.concatenate([growth[n : n + 1] * mass[:, piece] for n, piece in enumerate(lane_pieces(length))], axis=1)

    def step(n, carry):
        rows = pl.ds(pl.multiple_of(n * 256, 256), 256)
        weighted = kernel_ref[rows, :] * weight
        partial[rows, :] = sum(weighted[:, piece] for piece in lane_pieces(length))
        return carry

    lax.fori_loop(0, length // 256, step, 0)
    own_mass = got_ref[rank_ref[0], :, length:] * (1.0 / total)
    mine = own_piece(flat, rank_ref[0], own) + jnp.log(own_mass)
    pieces = [row_of_sums(partial[piece, :]) for piece in lane_pieces(length)]
    send = jnp.concatenate(pieces + [mine], axis=1)
    for d in range(groups):
        send_ref[d] = send


def column_sums_kernel(own, rank_ref, kernel_ref, got_ref, send_ref, mine_ref, columns, flat):
    groups = got_ref.shape[0]
    length = groups * own
    count = length // LANES
    logs = jnp.log(as_rows(jnp.sum(got_ref[:, :, :length], axis=0)))
    before = as_rows(last_rows(got_ref, length, own))
    potential = 0.5 * (before - logs)
    flat[:count, :] = potential
    flat[count:, :] = jnp.zeros((flat.shape[0] - count, LANES), jnp.float32)
    growth = jnp.exp(potential)
    store_columns([growth[n : n + 1] for n in range(count)], columns)

    def step(n, sums):
        rows = pl.ds(pl.multiple_of(n * 16, 16), 16)
        weighted = kernel_ref[rows, :] * repeated(columns[rows, :], length)
        return sums + (weighted[:8] + weighted[8:])

    sums = lax.fori_loop(0, length // 16, step, jnp.zeros((8, length), jnp.float32), unroll=4)
    sums = jnp.sum(sums, axis=0, keepdims=True)
    for d in range(groups):
        send_ref[d] = sums[:, d * own : (d + 1) * own]
    mine_ref[...] = own_piece(flat, rank_ref[1], own)[:, :own]


def shards(points, mass):
    own, width = points.shape
    groups = 16
    length = groups * own
    total = length * groups
    f32 = jnp.float32
    ranks = jnp.stack([lax.axis_index(ROW), lax.axis_index(COL)]).astype(jnp.int32)
    send, block = pl.pallas_call(
        functools.partial(copies_kernel, total),
        out_shape=[
            jax.ShapeDtypeStruct((groups, own, width), points.dtype),
            jax.ShapeDtypeStruct((2 * own + EXTRA, LANES), points.dtype),
        ],
        in_specs=[HBM, HBM],
        out_specs=[HBM, VMEM],
        scratch_shapes=[
            pltpu.VMEM((own, width), points.dtype),
            pltpu.VMEM((1, own), f32),
            pltpu.SemaphoreType.DMA((2,)),
            pltpu.SemaphoreType.DMA((groups,)),
        ],
        compiler_params=PARAMS,
    )(*(pltpu.with_memory_space_constraint(a, pltpu.HBM) for a in (points, mass.reshape(1, own))))
    left = lax.all_to_all(send, ROW, 0, 0)
    swap = [(0, 1), (1, 0)]
    pair = jnp.stack([block, lax.ppermute(block, "k", swap)])
    first = along_z(pair, 1)
    across = lax.ppermute(block, "z", [(z, z ^ 4) for z in range(8)])
    pair, first, across = lax.optimization_barrier((pair, first, across))
    side = jnp.concatenate([first, along_z(jnp.concatenate([pair, first]), 2), across[None]])
    far = lax.ppermute(side, "k", swap)
    ordered = [
        jax.ShapeDtypeStruct((groups, own, width), points.dtype),
        jax.ShapeDtypeStruct((groups, own, LANES), f32),
    ]
    right, columns, own_mass = pl.pallas_call(
        near_kernel,
        out_shape=ordered + [jax.ShapeDtypeStruct((1, LANES), f32)],
        in_specs=[SMEM, VMEM, VMEM],
        out_specs=[VMEM, VMEM, VMEM],
        compiler_params=PARAMS,
    )(ranks, pair, side)
    right, columns = pl.pallas_call(
        far_kernel,
        out_shape=ordered,
        in_specs=[SMEM, VMEM, VMEM, VMEM],
        out_specs=[VMEM, VMEM],
        input_output_aliases={2: 0, 3: 1},
        compiler_params=PARAMS,
    )(ranks, far, right, columns)
    message = jax.ShapeDtypeStruct((groups, 1, length + LANES), f32)
    kernel, send = pl.pallas_call(
        build_kernel,
        out_shape=[jax.ShapeDtypeStruct((length, length), f32), message],
        in_specs=[VMEM] * 4,
        out_specs=[VMEM, VMEM],
        compiler_params=PARAMS,
    )(right, columns, own_mass, left)
    got = lax.all_to_all(send, ROW, 0, 0)
    send = pl.pallas_call(
        functools.partial(row_sums_kernel, total, own),
        out_shape=message,
        in_specs=[SMEM, VMEM, VMEM],
        out_specs=VMEM,
        scratch_shapes=[pltpu.VMEM((length, LANES), f32), pltpu.VMEM((16, LANES), f32)],
        compiler_params=PARAMS,
    )(ranks, kernel, got)
    got = lax.all_to_all(send, COL, 0, 0)
    send, mine = pl.pallas_call(
        functools.partial(column_sums_kernel, own),
        out_shape=[jax.ShapeDtypeStruct((groups, 1, own), f32), jax.ShapeDtypeStruct((1, own), f32)],
        in_specs=[SMEM, VMEM, VMEM],
        out_specs=[VMEM, VMEM],
        scratch_shapes=[pltpu.VMEM((length, LANES), f32), pltpu.VMEM((16, LANES), f32)],
        compiler_params=PARAMS,
    )(ranks, kernel, got)
    sums = jnp.sum(lax.all_to_all(send, ROW, 0, 0), axis=0)
    return (0.5 * (mine - jnp.log(sums))).reshape(own)


def solution(mesh):
    fine = Mesh(mesh.devices.reshape(4, 2, 2, 2, 8), AXES)
    return jax.shard_map(
        shards,
        mesh=fine,
        in_specs=(P(AXES, None), P(AXES)),
        out_specs=P(AXES),
        check_vma=False,
    )
```

```python
import functools
import math

import jax
import jax.numpy as jnp
from jax import lax
from jax.experimental import pallas as pl
from jax.experimental.pallas import tpu as pltpu
from jax.sharding import Mesh
from jax.sharding import PartitionSpec as P

EPSILON = 0.1
AXES = ("x", "yl", "k", "yh", "z")
ROW = ("x", "yl", "yh")
COL = ("k", "z")
SIDE = ((1, 0), (1, 1), (2, 0), (2, 1), (3, 0), (3, 1), (4, 0))
LANES = 128
TILE = 512
ROWS = 768
EXTRA = 8
LOG2E = math.log2(math.e)
SCALE = LOG2E / EPSILON
VMEM = pl.BlockSpec(memory_space=pltpu.VMEM)
HBM = pl.BlockSpec(memory_space=pltpu.HBM)
SMEM = pl.BlockSpec(memory_space=pltpu.SMEM)
PARAMS = pltpu.CompilerParams(vmem_limit_bytes=40 * 2**20)


def lane_pieces(length):
    return [slice(n, n + LANES) for n in range(0, length, LANES)]


def store_columns(pieces, columns_ref):
    for n, piece in enumerate(pieces):
        columns_ref[n * LANES : (n + 1) * LANES, :] = jnp.broadcast_to(piece, (LANES, LANES)).T


def repeated(column, length):
    return jnp.concatenate([column] * (length // LANES), axis=1)


def row_of_sums(partial):
    return jnp.sum(partial.T, axis=0, keepdims=True)


def along_z(array, step):
    pairs = [(z, (z - step) % 8) for z in range(8)] + [(8 + z, 8 + (z + step) % 8) for z in range(8)]
    return lax.ppermute(array, ("k", "z"), pairs)


def three_parts(row):
    high = row.astype(jnp.bfloat16).astype(jnp.float32)
    middle = (row - high).astype(jnp.bfloat16).astype(jnp.float32)
    return [high, middle, row - high - middle]


def block_kernel(total, points_ref, mass_ref, block_ref, held, held_mass, read):
    own = points_ref.shape[0]
    reads = [pltpu.make_async_copy(points_ref, held, read.at[0]), pltpu.make_async_copy(mass_ref, held_mass, read.at[1])]
    for copy in reads:
        copy.start()
    for copy in reads:
        copy.wait()
    mass = held_mass[...]
    wide = held[...].astype(jnp.float32)
    halves = [wide[:, :LANES], wide[:, LANES:]]
    squares = halves[0] * halves[0] + halves[1] * halves[1]
    squares = jnp.concatenate([squares, jnp.zeros((LANES - own, LANES), jnp.float32)], axis=0)
    squares = row_of_sums(squares)[:, :own]
    base = LOG2E * jnp.log(mass * (1.0 / total)) - (0.5 * SCALE) * squares
    rows = three_parts(base) + three_parts(mass)
    rows.append(jnp.zeros((EXTRA - len(rows), own), jnp.float32))
    rows = jnp.concatenate(rows, axis=0)
    rows = jnp.concatenate([rows, jnp.zeros((EXTRA, LANES - own), jnp.float32)], axis=1)
    block_ref[...] = jnp.concatenate(halves + [rows], axis=0).astype(jnp.bfloat16)


def copies_kernel(block_ref, send_ref, held, written):
    own = held.shape[0]
    held[:, :LANES] = block_ref[:own, :]
    held[:, LANES:] = block_ref[own : 2 * own, :]
    copies = [pltpu.make_async_copy(held, send_ref.at[d], written.at[d]) for d in range(send_ref.shape[0])]
    for copy in copies:
        copy.start()
    for copy in copies:
        copy.wait()


def place_blocks(blocks_ref, places, core, z, right_ref, columns_ref):
    own = right_ref.shape[1]
    for n, (distance, other) in enumerate(places):
        place = 8 * (core ^ other) + ((z + (1 - 2 * core) * distance) & 7)
        right_ref[place, :, :LANES] = blocks_ref[n, :own, :]
        right_ref[place, :, LANES:] = blocks_ref[n, own : 2 * own, :]
        extra = blocks_ref[n].astype(jnp.float32)[2 * own :]
        base = jnp.sum(extra[0:3], axis=0, keepdims=True)
        columns_ref[place] = jnp.broadcast_to(base, (LANES, LANES)).T[:own]


def near_kernel(rank_ref, pair_ref, blocks_ref, right_ref, columns_ref, mass_ref):
    core, z = rank_ref[1] // 8, rank_ref[1] % 8
    place_blocks(pair_ref, ((0, 0), (0, 1)), core, z, right_ref, columns_ref)
    place_blocks(blocks_ref, SIDE, core, z, right_ref, columns_ref)
    extra = pair_ref[0].astype(jnp.float32)[2 * right_ref.shape[1] :]
    mass_ref[...] = jnp.sum(extra[3:6], axis=0, keepdims=True)


def far_kernel(rank_ref, blocks_ref, half_right_ref, half_columns_ref, right_ref, columns_ref):
    core, z = rank_ref[1] // 8, rank_ref[1] % 8
    place_blocks(blocks_ref, SIDE, 1 - core, z, right_ref, columns_ref)


def build_kernel(right_ref, columns_ref, mass_ref, left_ref, kernel_ref, send_ref):
    groups, own, width = left_ref.shape
    length = groups * own
    right = right_ref.reshape(length, width)
    columns = columns_ref.reshape(length, LANES)
    left = left_ref.reshape(length, width)
    sums = []
    for tile in range(0, length, TILE):
        squares = []
        for piece in range(tile, tile + TILE, LANES):
            wide = left[piece : piece + LANES, :].astype(jnp.float32)
            squares.append(row_of_sums(wide[:, :LANES] * wide[:, :LANES] + wide[:, LANES:] * wide[:, LANES:]))
        left_squares = (-0.5 * SCALE) * jnp.concatenate(squares, axis=1)
        total = jnp.zeros((8, TILE), jnp.float32)
        for start in range(0, length, ROWS):
            rows = slice(start, start + ROWS)
            inner = lax.dot_general(
                right[rows, :], left[tile : tile + TILE, :], (((1,), (1,)), ((), ())), preferred_element_type=jnp.float32
            )
            entries = jnp.exp2((SCALE * inner + left_squares) + repeated(columns[rows, :], TILE))
            kernel_ref[rows, tile : tile + TILE] = entries
            total = total + jnp.sum(entries.reshape(ROWS // 8, 8, TILE), axis=0)
        sums.append(jnp.sum(total, axis=0, keepdims=True))
    pieces = [total[:, piece] for total in sums for piece in lane_pieces(TILE)]
    send = jnp.concatenate(pieces + [mass_ref[...]], axis=1)
    for d in range(groups):
        send_ref[d] = send


def last_rows(got_ref, length, own):
    return jnp.concatenate([got_ref[d, :, length : length + own] for d in range(got_ref.shape[0])], axis=1)


def as_rows(row):
    return jnp.concatenate([row[:, piece] for piece in lane_pieces(row.shape[1])], axis=0)


def own_piece(flat_ref, rank, own):
    start = rank * own
    row, lane = start // LANES, start % LANES
    shift = (LANES - lane) % LANES
    first = pltpu.roll(jnp.broadcast_to(flat_ref[pl.ds(row, 1), :], (8, LANES)), shift, 1)
    second = pltpu.roll(jnp.broadcast_to(flat_ref[pl.ds(row + 1, 1), :], (8, LANES)), shift, 1)
    lanes = lax.broadcasted_iota(jnp.int32, (8, LANES), 1)
    return jnp.where(lanes < LANES - lane, first, second)[0:1]


def row_sums_kernel(total, own, rank_ref, kernel_ref, got_ref, send_ref, partial, flat):
    groups = got_ref.shape[0]
    length = groups * own
    count = length // LANES
    potential = -0.5 * jnp.log(as_rows(jnp.sum(got_ref[:, :, :length], axis=0)))
    flat[:count, :] = potential
    flat[count:, :] = jnp.zeros((flat.shape[0] - count, LANES), jnp.float32)
    growth = jnp.exp(potential)
    mass = last_rows(got_ref, length, own) * (1.0 / total)
    weight = jnp.concatenate([growth[n : n + 1] * mass[:, piece] for n, piece in enumerate(lane_pieces(length))], axis=1)

    def step(n, carry):
        rows = pl.ds(pl.multiple_of(n * 256, 256), 256)
        weighted = kernel_ref[rows, :] * weight
        partial[rows, :] = sum(weighted[:, piece] for piece in lane_pieces(length))
        return carry

    lax.fori_loop(0, length // 256, step, 0)
    own_mass = got_ref[rank_ref[0], :, length:] * (1.0 / total)
    mine = own_piece(flat, rank_ref[0], own) + jnp.log(own_mass)
    pieces = [row_of_sums(partial[piece, :]) for piece in lane_pieces(length)]
    send = jnp.concatenate(pieces + [mine], axis=1)
    for d in range(groups):
        send_ref[d] = send


def column_sums_kernel(own, rank_ref, kernel_ref, got_ref, send_ref, mine_ref, columns, flat):
    groups = got_ref.shape[0]
    length = groups * own
    count = length // LANES
    logs = jnp.log(as_rows(jnp.sum(got_ref[:, :, :length], axis=0)))
    before = as_rows(last_rows(got_ref, length, own))
    potential = 0.5 * (before - logs)
    flat[:count, :] = potential
    flat[count:, :] = jnp.zeros((flat.shape[0] - count, LANES), jnp.float32)
    growth = jnp.exp(potential)
    store_columns([growth[n : n + 1] for n in range(count)], columns)

    def step(n, sums):
        rows = pl.ds(pl.multiple_of(n * 16, 16), 16)
        weighted = kernel_ref[rows, :] * repeated(columns[rows, :], length)
        return sums + (weighted[:8] + weighted[8:])

    sums = lax.fori_loop(0, length // 16, step, jnp.zeros((8, length), jnp.float32), unroll=4)
    sums = jnp.sum(sums, axis=0, keepdims=True)
    for d in range(groups):
        send_ref[d] = sums[:, d * own : (d + 1) * own]
    mine_ref[...] = own_piece(flat, rank_ref[1], own)[:, :own]


def shards(points, mass):
    own, width = points.shape
    groups = 16
    length = groups * own
    total = length * groups
    f32 = jnp.float32
    ranks = jnp.stack([lax.axis_index(ROW), lax.axis_index(COL)]).astype(jnp.int32)
    block = pl.pallas_call(
        functools.partial(block_kernel, total),
        out_shape=jax.ShapeDtypeStruct((2 * own + EXTRA, LANES), points.dtype),
        in_specs=[HBM, HBM],
        out_specs=VMEM,
        scratch_shapes=[
            pltpu.VMEM((own, width), points.dtype),
            pltpu.VMEM((1, own), f32),
            pltpu.SemaphoreType.DMA((2,)),
        ],
        compiler_params=PARAMS,
    )(*(pltpu.with_memory_space_constraint(a, pltpu.HBM) for a in (points, mass.reshape(1, own))))
    send = pl.pallas_call(
        copies_kernel,
        out_shape=jax.ShapeDtypeStruct((groups, own, width), points.dtype),
        in_specs=[VMEM],
        out_specs=HBM,
        scratch_shapes=[pltpu.VMEM((own, width), points.dtype), pltpu.SemaphoreType.DMA((groups,))],
        compiler_params=PARAMS,
    )(block)
    swap = [(0, 1), (1, 0)]
    other, send = lax.optimization_barrier((lax.ppermute(block, "k", swap), send))
    pair = jnp.stack([block, other])
    first = along_z(pair, 1)
    across = lax.ppermute(block, "z", [(z, z ^ 4) for z in range(8)])
    pair, first, across = lax.optimization_barrier((pair, first, across))
    side = jnp.concatenate([first, along_z(jnp.concatenate([pair, first]), 2), across[None]])
    far = lax.ppermute(side, "k", swap)
    left = lax.all_to_all(send, ROW, 0, 0)
    ordered = [
        jax.ShapeDtypeStruct((groups, own, width), points.dtype),
        jax.ShapeDtypeStruct((groups, own, LANES), f32),
    ]
    right, columns, own_mass = pl.pallas_call(
        near_kernel,
        out_shape=ordered + [jax.ShapeDtypeStruct((1, LANES), f32)],
        in_specs=[SMEM, VMEM, VMEM],
        out_specs=[VMEM, VMEM, VMEM],
        compiler_params=PARAMS,
    )(ranks, pair, side)
    right, columns = pl.pallas_call(
        far_kernel,
        out_shape=ordered,
        in_specs=[SMEM, VMEM, VMEM, VMEM],
        out_specs=[VMEM, VMEM],
        input_output_aliases={2: 0, 3: 1},
        compiler_params=PARAMS,
    )(ranks, far, right, columns)
    message = jax.ShapeDtypeStruct((groups, 1, length + LANES), f32)
    kernel, send = pl.pallas_call(
        build_kernel,
        out_shape=[jax.ShapeDtypeStruct((length, length), f32), message],
        in_specs=[VMEM] * 4,
        out_specs=[VMEM, VMEM],
        compiler_params=PARAMS,
    )(right, columns, own_mass, left)
    got = lax.all_to_all(send, ROW, 0, 0)
    send = pl.pallas_call(
        functools.partial(row_sums_kernel, total, own),
        out_shape=message,
        in_specs=[SMEM, VMEM, VMEM],
        out_specs=VMEM,
        scratch_shapes=[pltpu.VMEM((length, LANES), f32), pltpu.VMEM((16, LANES), f32)],
        compiler_params=PARAMS,
    )(ranks, kernel, got)
    got = lax.all_to_all(send, COL, 0, 0)
    send, mine = pl.pallas_call(
        functools.partial(column_sums_kernel, own),
        out_shape=[jax.ShapeDtypeStruct((groups, 1, own), f32), jax.ShapeDtypeStruct((1, own), f32)],
        in_specs=[SMEM, VMEM, VMEM],
        out_specs=[VMEM, VMEM],
        scratch_shapes=[pltpu.VMEM((length, LANES), f32), pltpu.VMEM((16, LANES), f32)],
        compiler_params=PARAMS,
    )(ranks, kernel, got)
    sums = jnp.sum(lax.all_to_all(send, ROW, 0, 0), axis=0)
    return (0.5 * (mine - jnp.log(sums))).reshape(own)


def solution(mesh):
    fine = Mesh(mesh.devices.reshape(4, 2, 2, 2, 8), AXES)
    return jax.shard_map(
        shards,
        mesh=fine,
        in_specs=(P(AXES, None), P(AXES)),
        out_specs=P(AXES),
        check_vma=False,
    )
```

```python
import functools
import math

import jax
import jax.numpy as jnp
from jax import lax
from jax.experimental import pallas as pl
from jax.experimental.pallas import tpu as pltpu
from jax.sharding import Mesh
from jax.sharding import PartitionSpec as P

EPSILON = 0.1
AXES = ("x", "yl", "k", "yh", "z")
ROW = ("x", "yl", "yh")
COL = ("k", "z")
SIDE = ((2, 0), (2, 1), (1, 0), (1, 1), (3, 0), (3, 1), (4, 0))
LANES = 128
TILE = 512
ROWS = 768
EXTRA = 8
LOG2E = math.log2(math.e)
SCALE = LOG2E / EPSILON
VMEM = pl.BlockSpec(memory_space=pltpu.VMEM)
HBM = pl.BlockSpec(memory_space=pltpu.HBM)
SMEM = pl.BlockSpec(memory_space=pltpu.SMEM)
PARAMS = pltpu.CompilerParams(vmem_limit_bytes=40 * 2**20)


def lane_pieces(length):
    return [slice(n, n + LANES) for n in range(0, length, LANES)]


def store_columns(pieces, columns_ref):
    for n, piece in enumerate(pieces):
        columns_ref[n * LANES : (n + 1) * LANES, :] = jnp.broadcast_to(piece, (LANES, LANES)).T


def repeated(column, length):
    return jnp.concatenate([column] * (length // LANES), axis=1)


def row_of_sums(partial):
    return jnp.sum(partial.T, axis=0, keepdims=True)


def along_z(array, step):
    pairs = [(z, (z - step) % 8) for z in range(8)] + [(8 + z, 8 + (z + step) % 8) for z in range(8)]
    return lax.ppermute(array, ("k", "z"), pairs)


def three_parts(row):
    high = row.astype(jnp.bfloat16).astype(jnp.float32)
    middle = (row - high).astype(jnp.bfloat16).astype(jnp.float32)
    return [high, middle, row - high - middle]


def block_kernel(total, points_ref, mass_ref, block_ref, held, held_mass, read):
    own = points_ref.shape[0]
    reads = [pltpu.make_async_copy(points_ref, held, read.at[0]), pltpu.make_async_copy(mass_ref, held_mass, read.at[1])]
    for copy in reads:
        copy.start()
    for copy in reads:
        copy.wait()
    mass = held_mass[...]
    wide = held[...].astype(jnp.float32)
    halves = [wide[:, :LANES], wide[:, LANES:]]
    squares = halves[0] * halves[0] + halves[1] * halves[1]
    squares = jnp.concatenate([squares, jnp.zeros((LANES - own, LANES), jnp.float32)], axis=0)
    squares = row_of_sums(squares)[:, :own]
    base = LOG2E * jnp.log(mass * (1.0 / total)) - (0.5 * SCALE) * squares
    rows = three_parts(base) + three_parts(mass)
    rows.append(jnp.zeros((EXTRA - len(rows), own), jnp.float32))
    rows = jnp.concatenate(rows, axis=0)
    rows = jnp.concatenate([rows, jnp.zeros((EXTRA, LANES - own), jnp.float32)], axis=1)
    block_ref[...] = jnp.concatenate(halves + [rows], axis=0).astype(jnp.bfloat16)


def copies_kernel(block_ref, send_ref, held, written):
    own = held.shape[0]
    held[:, :LANES] = block_ref[:own, :]
    held[:, LANES:] = block_ref[own : 2 * own, :]
    copies = [pltpu.make_async_copy(held, send_ref.at[d], written.at[d]) for d in range(send_ref.shape[0])]
    for copy in copies:
        copy.start()
    for copy in copies:
        copy.wait()


def place_blocks(blocks_ref, places, core, z, right_ref, columns_ref):
    own = right_ref.shape[1]
    for n, (distance, other) in enumerate(places):
        place = 8 * (core ^ other) + ((z + (1 - 2 * core) * distance) & 7)
        right_ref[place, :, :LANES] = blocks_ref[n, :own, :]
        right_ref[place, :, LANES:] = blocks_ref[n, own : 2 * own, :]
        extra = blocks_ref[n].astype(jnp.float32)[2 * own :]
        base = jnp.sum(extra[0:3], axis=0, keepdims=True)
        columns_ref[place] = jnp.broadcast_to(base, (LANES, LANES)).T[:own]


def near_kernel(rank_ref, pair_ref, blocks_ref, right_ref, columns_ref, mass_ref):
    core, z = rank_ref[1] // 8, rank_ref[1] % 8
    place_blocks(pair_ref, ((0, 0), (0, 1)), core, z, right_ref, columns_ref)
    place_blocks(blocks_ref, SIDE, core, z, right_ref, columns_ref)
    extra = pair_ref[0].astype(jnp.float32)[2 * right_ref.shape[1] :]
    mass_ref[...] = jnp.sum(extra[3:6], axis=0, keepdims=True)


def far_kernel(rank_ref, blocks_ref, half_right_ref, half_columns_ref, right_ref, columns_ref):
    core, z = rank_ref[1] // 8, rank_ref[1] % 8
    place_blocks(blocks_ref, SIDE, 1 - core, z, right_ref, columns_ref)


def build_kernel(right_ref, columns_ref, mass_ref, left_ref, kernel_ref, send_ref):
    groups, own, width = left_ref.shape
    length = groups * own
    right = right_ref.reshape(length, width)
    columns = columns_ref.reshape(length, LANES)
    left = left_ref.reshape(length, width)
    sums = []
    for tile in range(0, length, TILE):
        squares = []
        for piece in range(tile, tile + TILE, LANES):
            wide = left[piece : piece + LANES, :].astype(jnp.float32)
            squares.append(row_of_sums(wide[:, :LANES] * wide[:, :LANES] + wide[:, LANES:] * wide[:, LANES:]))
        left_squares = (-0.5 * SCALE) * jnp.concatenate(squares, axis=1)
        total = jnp.zeros((8, TILE), jnp.float32)
        for start in range(0, length, ROWS):
            rows = slice(start, start + ROWS)
            inner = lax.dot_general(
                right[rows, :], left[tile : tile + TILE, :], (((1,), (1,)), ((), ())), preferred_element_type=jnp.float32
            )
            entries = jnp.exp2((SCALE * inner + left_squares) + repeated(columns[rows, :], TILE))
            kernel_ref[rows, tile : tile + TILE] = entries
            total = total + jnp.sum(entries.reshape(ROWS // 8, 8, TILE), axis=0)
        sums.append(jnp.sum(total, axis=0, keepdims=True))
    pieces = [total[:, piece] for total in sums for piece in lane_pieces(TILE)]
    send = jnp.concatenate(pieces + [mass_ref[...]], axis=1)
    for d in range(groups):
        send_ref[d] = send


def last_rows(got_ref, length, own):
    return jnp.concatenate([got_ref[d, :, length : length + own] for d in range(got_ref.shape[0])], axis=1)


def as_rows(row):
    return jnp.concatenate([row[:, piece] for piece in lane_pieces(row.shape[1])], axis=0)


def own_piece(flat_ref, rank, own):
    start = rank * own
    row, lane = start // LANES, start % LANES
    shift = (LANES - lane) % LANES
    first = pltpu.roll(jnp.broadcast_to(flat_ref[pl.ds(row, 1), :], (8, LANES)), shift, 1)
    second = pltpu.roll(jnp.broadcast_to(flat_ref[pl.ds(row + 1, 1), :], (8, LANES)), shift, 1)
    lanes = lax.broadcasted_iota(jnp.int32, (8, LANES), 1)
    return jnp.where(lanes < LANES - lane, first, second)[0:1]


def row_sums_kernel(total, own, rank_ref, kernel_ref, got_ref, send_ref, partial, flat):
    groups = got_ref.shape[0]
    length = groups * own
    count = length // LANES
    potential = -0.5 * jnp.log(as_rows(jnp.sum(got_ref[:, :, :length], axis=0)))
    flat[:count, :] = potential
    flat[count:, :] = jnp.zeros((flat.shape[0] - count, LANES), jnp.float32)
    growth = jnp.exp(potential)
    mass = last_rows(got_ref, length, own) * (1.0 / total)
    weight = jnp.concatenate([growth[n : n + 1] * mass[:, piece] for n, piece in enumerate(lane_pieces(length))], axis=1)

    def step(n, carry):
        rows = pl.ds(pl.multiple_of(n * 256, 256), 256)
        weighted = kernel_ref[rows, :] * weight
        partial[rows, :] = sum(weighted[:, piece] for piece in lane_pieces(length))
        return carry

    lax.fori_loop(0, length // 256, step, 0)
    own_mass = got_ref[rank_ref[0], :, length:] * (1.0 / total)
    mine = own_piece(flat, rank_ref[0], own) + jnp.log(own_mass)
    pieces = [row_of_sums(partial[piece, :]) for piece in lane_pieces(length)]
    send = jnp.concatenate(pieces + [mine], axis=1)
    for d in range(groups):
        send_ref[d] = send


def column_sums_kernel(own, rank_ref, kernel_ref, got_ref, send_ref, mine_ref, columns, flat):
    groups = got_ref.shape[0]
    length = groups * own
    count = length // LANES
    logs = jnp.log(as_rows(jnp.sum(got_ref[:, :, :length], axis=0)))
    before = as_rows(last_rows(got_ref, length, own))
    potential = 0.5 * (before - logs)
    flat[:count, :] = potential
    flat[count:, :] = jnp.zeros((flat.shape[0] - count, LANES), jnp.float32)
    growth = jnp.exp(potential)
    store_columns([growth[n : n + 1] for n in range(count)], columns)

    def step(n, sums):
        rows = pl.ds(pl.multiple_of(n * 16, 16), 16)
        weighted = kernel_ref[rows, :] * repeated(columns[rows, :], length)
        return sums + (weighted[:8] + weighted[8:])

    sums = lax.fori_loop(0, length // 16, step, jnp.zeros((8, length), jnp.float32), unroll=4)
    sums = jnp.sum(sums, axis=0, keepdims=True)
    for d in range(groups):
        send_ref[d] = sums[:, d * own : (d + 1) * own]
    mine_ref[...] = own_piece(flat, rank_ref[1], own)[:, :own]


def shards(points, mass):
    own, width = points.shape
    groups = 16
    length = groups * own
    total = length * groups
    f32 = jnp.float32
    ranks = jnp.stack([lax.axis_index(ROW), lax.axis_index(COL)]).astype(jnp.int32)
    block = pl.pallas_call(
        functools.partial(block_kernel, total),
        out_shape=jax.ShapeDtypeStruct((2 * own + EXTRA, LANES), points.dtype),
        in_specs=[HBM, HBM],
        out_specs=VMEM,
        scratch_shapes=[
            pltpu.VMEM((own, width), points.dtype),
            pltpu.VMEM((1, own), f32),
            pltpu.SemaphoreType.DMA((2,)),
        ],
        compiler_params=PARAMS,
    )(*(pltpu.with_memory_space_constraint(a, pltpu.HBM) for a in (points, mass.reshape(1, own))))
    send = pl.pallas_call(
        copies_kernel,
        out_shape=jax.ShapeDtypeStruct((groups, own, width), points.dtype),
        in_specs=[VMEM],
        out_specs=HBM,
        scratch_shapes=[pltpu.VMEM((own, width), points.dtype), pltpu.SemaphoreType.DMA((groups,))],
        compiler_params=PARAMS,
    )(block)
    swap = [(0, 1), (1, 0)]
    other, send = lax.optimization_barrier((lax.ppermute(block, "k", swap), send))
    pair = jnp.stack([block, other])
    first = along_z(pair, 2)
    across = lax.ppermute(block, "z", [(z, z ^ 4) for z in range(8)])
    side = jnp.concatenate([first, along_z(jnp.concatenate([pair, first]), 1), across[None]])
    far = lax.ppermute(side, "k", swap)
    left = lax.all_to_all(send, ROW, 0, 0)
    ordered = [
        jax.ShapeDtypeStruct((groups, own, width), points.dtype),
        jax.ShapeDtypeStruct((groups, own, LANES), f32),
    ]
    right, columns, own_mass = pl.pallas_call(
        near_kernel,
        out_shape=ordered + [jax.ShapeDtypeStruct((1, LANES), f32)],
        in_specs=[SMEM, VMEM, VMEM],
        out_specs=[VMEM, VMEM, VMEM],
        compiler_params=PARAMS,
    )(ranks, pair, side)
    right, columns = pl.pallas_call(
        far_kernel,
        out_shape=ordered,
        in_specs=[SMEM, VMEM, VMEM, VMEM],
        out_specs=[VMEM, VMEM],
        input_output_aliases={2: 0, 3: 1},
        compiler_params=PARAMS,
    )(ranks, far, right, columns)
    message = jax.ShapeDtypeStruct((groups, 1, length + LANES), f32)
    kernel, send = pl.pallas_call(
        build_kernel,
        out_shape=[jax.ShapeDtypeStruct((length, length), f32), message],
        in_specs=[VMEM] * 4,
        out_specs=[VMEM, VMEM],
        compiler_params=PARAMS,
    )(right, columns, own_mass, left)
    got = lax.all_to_all(send, ROW, 0, 0)
    send = pl.pallas_call(
        functools.partial(row_sums_kernel, total, own),
        out_shape=message,
        in_specs=[SMEM, VMEM, VMEM],
        out_specs=VMEM,
        scratch_shapes=[pltpu.VMEM((length, LANES), f32), pltpu.VMEM((16, LANES), f32)],
        compiler_params=PARAMS,
    )(ranks, kernel, got)
    got = lax.all_to_all(send, COL, 0, 0)
    send, mine = pl.pallas_call(
        functools.partial(column_sums_kernel, own),
        out_shape=[jax.ShapeDtypeStruct((groups, 1, own), f32), jax.ShapeDtypeStruct((1, own), f32)],
        in_specs=[SMEM, VMEM, VMEM],
        out_specs=[VMEM, VMEM],
        scratch_shapes=[pltpu.VMEM((length, LANES), f32), pltpu.VMEM((16, LANES), f32)],
        compiler_params=PARAMS,
    )(ranks, kernel, got)
    sums = jnp.sum(lax.all_to_all(send, ROW, 0, 0), axis=0)
    return (0.5 * (mine - jnp.log(sums))).reshape(own)


def solution(mesh):
    fine = Mesh(mesh.devices.reshape(4, 2, 2, 2, 8), AXES)
    return jax.shard_map(
        shards,
        mesh=fine,
        in_specs=(P(AXES, None), P(AXES)),
        out_specs=P(AXES),
        check_vma=False,
    )
```

```python
import functools
import math

import jax
import jax.numpy as jnp
from jax import lax
from jax.experimental import pallas as pl
from jax.experimental.pallas import tpu as pltpu
from jax.sharding import Mesh
from jax.sharding import PartitionSpec as P

EPSILON = 0.1
AXES = ("x", "yl", "k", "yh", "z")
ROW = ("x", "yl", "yh")
COL = ("k", "z")
SIDE = ((2, 0), (2, 1), (1, 0), (1, 1), (3, 0), (3, 1))
LANES = 128
TILE = 512
ROWS = 768
EXTRA = 8
LOG2E = math.log2(math.e)
SCALE = LOG2E / EPSILON
VMEM = pl.BlockSpec(memory_space=pltpu.VMEM)
HBM = pl.BlockSpec(memory_space=pltpu.HBM)
SMEM = pl.BlockSpec(memory_space=pltpu.SMEM)
PARAMS = pltpu.CompilerParams(vmem_limit_bytes=40 * 2**20)


def lane_pieces(length):
    return [slice(n, n + LANES) for n in range(0, length, LANES)]


def store_columns(pieces, columns_ref):
    for n, piece in enumerate(pieces):
        columns_ref[n * LANES : (n + 1) * LANES, :] = jnp.broadcast_to(piece, (LANES, LANES)).T


def repeated(column, length):
    return jnp.concatenate([column] * (length // LANES), axis=1)


def row_of_sums(partial):
    return jnp.sum(partial.T, axis=0, keepdims=True)


def along_z(array, step):
    pairs = [(z, (z - step) % 8) for z in range(8)] + [(8 + z, 8 + (z + step) % 8) for z in range(8)]
    return lax.ppermute(array, ("k", "z"), pairs)


def three_parts(row):
    high = row.astype(jnp.bfloat16).astype(jnp.float32)
    middle = (row - high).astype(jnp.bfloat16).astype(jnp.float32)
    return [high, middle, row - high - middle]


def block_kernel(total, points_ref, mass_ref, block_ref, held, held_mass, read):
    own = points_ref.shape[0]
    reads = [pltpu.make_async_copy(points_ref, held, read.at[0]), pltpu.make_async_copy(mass_ref, held_mass, read.at[1])]
    for copy in reads:
        copy.start()
    for copy in reads:
        copy.wait()
    mass = held_mass[...]
    wide = held[...].astype(jnp.float32)
    halves = [wide[:, :LANES], wide[:, LANES:]]
    squares = halves[0] * halves[0] + halves[1] * halves[1]
    squares = jnp.concatenate([squares, jnp.zeros((LANES - own, LANES), jnp.float32)], axis=0)
    squares = row_of_sums(squares)[:, :own]
    base = LOG2E * jnp.log(mass * (1.0 / total)) - (0.5 * SCALE) * squares
    rows = three_parts(base) + three_parts(mass)
    rows.append(jnp.zeros((EXTRA - len(rows), own), jnp.float32))
    rows = jnp.concatenate(rows, axis=0)
    rows = jnp.concatenate([rows, jnp.zeros((EXTRA, LANES - own), jnp.float32)], axis=1)
    block_ref[...] = jnp.concatenate(halves + [rows], axis=0).astype(jnp.bfloat16)


def copies_kernel(block_ref, send_ref, held, written):
    own = held.shape[0]
    held[:, :LANES] = block_ref[:own, :]
    held[:, LANES:] = block_ref[own : 2 * own, :]
    copies = [pltpu.make_async_copy(held, send_ref.at[d], written.at[d]) for d in range(send_ref.shape[0])]
    for copy in copies:
        copy.start()
    for copy in copies:
        copy.wait()


def place_blocks(blocks_ref, places, core, z, right_ref, columns_ref):
    own = right_ref.shape[1]
    for n, (distance, other) in enumerate(places):
        place = 8 * (core ^ other) + ((z + (1 - 2 * core) * distance) & 7)
        right_ref[place, :, :LANES] = blocks_ref[n, :own, :]
        right_ref[place, :, LANES:] = blocks_ref[n, own : 2 * own, :]
        extra = blocks_ref[n].astype(jnp.float32)[2 * own :]
        base = jnp.sum(extra[0:3], axis=0, keepdims=True)
        columns_ref[place] = jnp.broadcast_to(base, (LANES, LANES)).T[:own]


def near_kernel(rank_ref, pair_ref, blocks_ref, right_ref, columns_ref, mass_ref):
    core, z = rank_ref[1] // 8, rank_ref[1] % 8
    place_blocks(pair_ref, ((0, 0), (0, 1)), core, z, right_ref, columns_ref)
    place_blocks(blocks_ref, SIDE, core, z, right_ref, columns_ref)
    extra = pair_ref[0].astype(jnp.float32)[2 * right_ref.shape[1] :]
    mass_ref[...] = jnp.sum(extra[3:6], axis=0, keepdims=True)


def far_kernel(rank_ref, blocks_ref, last_ref, half_right_ref, half_columns_ref, right_ref, columns_ref):
    core, z = rank_ref[1] // 8, rank_ref[1] % 8
    place_blocks(last_ref, ((4, 0), (4, 1)), core, z, right_ref, columns_ref)
    place_blocks(blocks_ref, SIDE, 1 - core, z, right_ref, columns_ref)


def build_kernel(right_ref, columns_ref, mass_ref, left_ref, kernel_ref, send_ref):
    groups, own, width = left_ref.shape
    length = groups * own
    right = right_ref.reshape(length, width)
    columns = columns_ref.reshape(length, LANES)
    left = left_ref.reshape(length, width)
    sums = []
    for tile in range(0, length, TILE):
        squares = []
        for piece in range(tile, tile + TILE, LANES):
            wide = left[piece : piece + LANES, :].astype(jnp.float32)
            squares.append(row_of_sums(wide[:, :LANES] * wide[:, :LANES] + wide[:, LANES:] * wide[:, LANES:]))
        left_squares = (-0.5 * SCALE) * jnp.concatenate(squares, axis=1)
        total = jnp.zeros((8, TILE), jnp.float32)
        for start in range(0, length, ROWS):
            rows = slice(start, start + ROWS)
            inner = lax.dot_general(
                right[rows, :], left[tile : tile + TILE, :], (((1,), (1,)), ((), ())), preferred_element_type=jnp.float32
            )
            entries = jnp.exp2((SCALE * inner + left_squares) + repeated(columns[rows, :], TILE))
            kernel_ref[rows, tile : tile + TILE] = entries
            total = total + jnp.sum(entries.reshape(ROWS // 8, 8, TILE), axis=0)
        sums.append(jnp.sum(total, axis=0, keepdims=True))
    pieces = [total[:, piece] for total in sums for piece in lane_pieces(TILE)]
    send = jnp.concatenate(pieces + [mass_ref[...]], axis=1)
    for d in range(groups):
        send_ref[d] = send


def last_rows(got_ref, length, own):
    return jnp.concatenate([got_ref[d, :, length : length + own] for d in range(got_ref.shape[0])], axis=1)


def as_rows(row):
    return jnp.concatenate([row[:, piece] for piece in lane_pieces(row.shape[1])], axis=0)


def own_piece(flat_ref, rank, own):
    start = rank * own
    row, lane = start // LANES, start % LANES
    shift = (LANES - lane) % LANES
    first = pltpu.roll(jnp.broadcast_to(flat_ref[pl.ds(row, 1), :], (8, LANES)), shift, 1)
    second = pltpu.roll(jnp.broadcast_to(flat_ref[pl.ds(row + 1, 1), :], (8, LANES)), shift, 1)
    lanes = lax.broadcasted_iota(jnp.int32, (8, LANES), 1)
    return jnp.where(lanes < LANES - lane, first, second)[0:1]


def row_sums_kernel(total, own, rank_ref, kernel_ref, got_ref, send_ref, partial, flat):
    groups = got_ref.shape[0]
    length = groups * own
    count = length // LANES
    potential = -0.5 * jnp.log(as_rows(jnp.sum(got_ref[:, :, :length], axis=0)))
    flat[:count, :] = potential
    flat[count:, :] = jnp.zeros((flat.shape[0] - count, LANES), jnp.float32)
    growth = jnp.exp(potential)
    mass = last_rows(got_ref, length, own) * (1.0 / total)
    weight = jnp.concatenate([growth[n : n + 1] * mass[:, piece] for n, piece in enumerate(lane_pieces(length))], axis=1)

    def step(n, carry):
        rows = pl.ds(pl.multiple_of(n * 512, 512), 512)
        weighted = kernel_ref[rows, :] * weight
        partial[rows, :] = sum(weighted[:, piece] for piece in lane_pieces(length))
        return carry

    lax.fori_loop(0, length // 512, step, 0)
    own_mass = got_ref[rank_ref[0], :, length:] * (1.0 / total)
    mine = own_piece(flat, rank_ref[0], own) + jnp.log(own_mass)
    pieces = [row_of_sums(partial[piece, :]) for piece in lane_pieces(length)]
    send = jnp.concatenate(pieces + [mine], axis=1)
    for d in range(groups):
        send_ref[d] = send


def column_sums_kernel(own, rank_ref, kernel_ref, got_ref, send_ref, mine_ref, columns, flat):
    groups = got_ref.shape[0]
    length = groups * own
    count = length // LANES
    logs = jnp.log(as_rows(jnp.sum(got_ref[:, :, :length], axis=0)))
    before = as_rows(last_rows(got_ref, length, own))
    potential = 0.5 * (before - logs)
    flat[:count, :] = potential
    flat[count:, :] = jnp.zeros((flat.shape[0] - count, LANES), jnp.float32)
    growth = jnp.exp(potential)
    store_columns([growth[n : n + 1] for n in range(count)], columns)

    def step(n, sums):
        rows = pl.ds(pl.multiple_of(n * 16, 16), 16)
        weighted = kernel_ref[rows, :] * repeated(columns[rows, :], length)
        return sums + (weighted[:8] + weighted[8:])

    sums = lax.fori_loop(0, length // 16, step, jnp.zeros((8, length), jnp.float32), unroll=8)
    sums = jnp.sum(sums, axis=0, keepdims=True)
    for d in range(groups):
        send_ref[d] = sums[:, d * own : (d + 1) * own]
    mine_ref[...] = own_piece(flat, rank_ref[1], own)[:, :own]


def shards(points, mass):
    own, width = points.shape
    groups = 16
    length = groups * own
    total = length * groups
    f32 = jnp.float32
    ranks = jnp.stack([lax.axis_index(ROW), lax.axis_index(COL)]).astype(jnp.int32)
    block = pl.pallas_call(
        functools.partial(block_kernel, total),
        out_shape=jax.ShapeDtypeStruct((2 * own + EXTRA, LANES), points.dtype),
        in_specs=[HBM, HBM],
        out_specs=VMEM,
        scratch_shapes=[
            pltpu.VMEM((own, width), points.dtype),
            pltpu.VMEM((1, own), f32),
            pltpu.SemaphoreType.DMA((2,)),
        ],
        compiler_params=PARAMS,
    )(*(pltpu.with_memory_space_constraint(a, pltpu.HBM) for a in (points, mass.reshape(1, own))))
    send = pl.pallas_call(
        copies_kernel,
        out_shape=jax.ShapeDtypeStruct((groups, own, width), points.dtype),
        in_specs=[VMEM],
        out_specs=HBM,
        scratch_shapes=[pltpu.VMEM((own, width), points.dtype), pltpu.SemaphoreType.DMA((groups,))],
        compiler_params=PARAMS,
    )(block)
    swap = [(0, 1), (1, 0)]
    other, send = lax.optimization_barrier((lax.ppermute(block, "k", swap), send))
    pair = jnp.stack([block, other])
    first = along_z(pair, 2)
    last, second = along_z(first, 2), along_z(jnp.concatenate([pair, first]), 1)
    last, second = lax.optimization_barrier((last, second))
    side = jnp.concatenate([first, second])
    far = lax.ppermute(side, "k", swap)
    left = lax.all_to_all(send, ROW, 0, 0)
    ordered = [
        jax.ShapeDtypeStruct((groups, own, width), points.dtype),
        jax.ShapeDtypeStruct((groups, own, LANES), f32),
    ]
    right, columns, own_mass = pl.pallas_call(
        near_kernel,
        out_shape=ordered + [jax.ShapeDtypeStruct((1, LANES), f32)],
        in_specs=[SMEM, VMEM, VMEM],
        out_specs=[VMEM, VMEM, VMEM],
        compiler_params=PARAMS,
    )(ranks, pair, side)
    right, columns = pl.pallas_call(
        far_kernel,
        out_shape=ordered,
        in_specs=[SMEM] + [VMEM] * 4,
        out_specs=[VMEM, VMEM],
        input_output_aliases={3: 0, 4: 1},
        compiler_params=PARAMS,
    )(ranks, far, last, right, columns)
    message = jax.ShapeDtypeStruct((groups, 1, length + LANES), f32)
    kernel, send = pl.pallas_call(
        build_kernel,
        out_shape=[jax.ShapeDtypeStruct((length, length), f32), message],
        in_specs=[VMEM] * 4,
        out_specs=[VMEM, VMEM],
        compiler_params=PARAMS,
    )(right, columns, own_mass, left)
    got = lax.all_to_all(send, ROW, 0, 0)
    send = pl.pallas_call(
        functools.partial(row_sums_kernel, total, own),
        out_shape=message,
        in_specs=[SMEM, VMEM, VMEM],
        out_specs=VMEM,
        scratch_shapes=[pltpu.VMEM((length, LANES), f32), pltpu.VMEM((16, LANES), f32)],
        compiler_params=PARAMS,
    )(ranks, kernel, got)
    got = lax.all_to_all(send, COL, 0, 0)
    send, mine = pl.pallas_call(
        functools.partial(column_sums_kernel, own),
        out_shape=[jax.ShapeDtypeStruct((groups, 1, own), f32), jax.ShapeDtypeStruct((1, own), f32)],
        in_specs=[SMEM, VMEM, VMEM],
        out_specs=[VMEM, VMEM],
        scratch_shapes=[pltpu.VMEM((length, LANES), f32), pltpu.VMEM((16, LANES), f32)],
        compiler_params=PARAMS,
    )(ranks, kernel, got)
    sums = jnp.sum(lax.all_to_all(send, ROW, 0, 0), axis=0)
    return (0.5 * (mine - jnp.log(sums))).reshape(own)


def solution(mesh):
    fine = Mesh(mesh.devices.reshape(4, 2, 2, 2, 8), AXES)
    return jax.shard_map(
        shards,
        mesh=fine,
        in_specs=(P(AXES, None), P(AXES)),
        out_specs=P(AXES),
        check_vma=False,
    )
```

```python
import functools
import math

import jax
import jax.numpy as jnp
from jax import lax
from jax.experimental import pallas as pl
from jax.experimental.pallas import tpu as pltpu
from jax.sharding import Mesh
from jax.sharding import PartitionSpec as P

EPSILON = 0.1
AXES = ("x", "yl", "k", "yh", "z")
ROW = ("x", "yl", "yh")
COL = ("k", "z")
SIDE = ((2, 0), (2, 1), (1, 0), (1, 1), (3, 0), (3, 1))
LANES = 128
TILE = 512
ROWS = 768
EXTRA = 8
LOG2E = math.log2(math.e)
SCALE = LOG2E / EPSILON
VMEM = pl.BlockSpec(memory_space=pltpu.VMEM)
HBM = pl.BlockSpec(memory_space=pltpu.HBM)
SMEM = pl.BlockSpec(memory_space=pltpu.SMEM)
PARAMS = pltpu.CompilerParams(vmem_limit_bytes=40 * 2**20)


def lane_pieces(length):
    return [slice(n, n + LANES) for n in range(0, length, LANES)]


def store_columns(pieces, columns_ref):
    for n, piece in enumerate(pieces):
        columns_ref[n * LANES : (n + 1) * LANES, :] = jnp.broadcast_to(piece, (LANES, LANES)).T


def repeated(column, length):
    return jnp.concatenate([column] * (length // LANES), axis=1)


def row_of_sums(partial):
    return jnp.sum(partial.T, axis=0, keepdims=True)


def along_z(array, step):
    pairs = [(z, (z - step) % 8) for z in range(8)] + [(8 + z, 8 + (z + step) % 8) for z in range(8)]
    return lax.ppermute(array, ("k", "z"), pairs)


def three_parts(row):
    high = row.astype(jnp.bfloat16).astype(jnp.float32)
    middle = (row - high).astype(jnp.bfloat16).astype(jnp.float32)
    return [high, middle, row - high - middle]


def block_kernel(total, points_ref, mass_ref, block_ref, held, held_mass, read):
    own = points_ref.shape[0]
    reads = [pltpu.make_async_copy(points_ref, held, read.at[0]), pltpu.make_async_copy(mass_ref, held_mass, read.at[1])]
    for copy in reads:
        copy.start()
    for copy in reads:
        copy.wait()
    mass = held_mass[...]
    wide = held[...].astype(jnp.float32)
    halves = [wide[:, :LANES], wide[:, LANES:]]
    squares = halves[0] * halves[0] + halves[1] * halves[1]
    squares = jnp.concatenate([squares, jnp.zeros((LANES - own, LANES), jnp.float32)], axis=0)
    squares = row_of_sums(squares)[:, :own]
    base = LOG2E * jnp.log(mass * (1.0 / total)) - (0.5 * SCALE) * squares
    rows = three_parts(base) + three_parts(mass)
    rows.append(jnp.zeros((EXTRA - len(rows), own), jnp.float32))
    rows = jnp.concatenate(rows, axis=0)
    rows = jnp.concatenate([rows, jnp.zeros((EXTRA, LANES - own), jnp.float32)], axis=1)
    block_ref[...] = jnp.concatenate(halves + [rows], axis=0).astype(jnp.bfloat16)


def copies_kernel(block_ref, send_ref, held, written):
    own = held.shape[0]
    held[:, :LANES] = block_ref[:own, :]
    held[:, LANES:] = block_ref[own : 2 * own, :]
    copies = [pltpu.make_async_copy(held, send_ref.at[d], written.at[d]) for d in range(send_ref.shape[0])]
    for copy in copies:
        copy.start()
    for copy in copies:
        copy.wait()


def place_blocks(blocks_ref, places, core, z, right_ref, columns_ref):
    own = right_ref.shape[1]
    for n, (distance, other) in enumerate(places):
        place = 8 * (core ^ other) + ((z + (1 - 2 * core) * distance) & 7)
        right_ref[place, :, :LANES] = blocks_ref[n, :own, :]
        right_ref[place, :, LANES:] = blocks_ref[n, own : 2 * own, :]
        extra = blocks_ref[n].astype(jnp.float32)[2 * own :]
        base = jnp.sum(extra[0:3], axis=0, keepdims=True)
        columns_ref[place] = jnp.broadcast_to(base, (LANES, LANES)).T[:own]


def near_kernel(rank_ref, pair_ref, blocks_ref, right_ref, columns_ref, mass_ref):
    core, z = rank_ref[1] // 8, rank_ref[1] % 8
    place_blocks(pair_ref, ((0, 0), (0, 1)), core, z, right_ref, columns_ref)
    place_blocks(blocks_ref, SIDE, core, z, right_ref, columns_ref)
    extra = pair_ref[0].astype(jnp.float32)[2 * right_ref.shape[1] :]
    mass_ref[...] = jnp.sum(extra[3:6], axis=0, keepdims=True)


def far_kernel(rank_ref, blocks_ref, last_ref, half_right_ref, half_columns_ref, right_ref, columns_ref):
    core, z = rank_ref[1] // 8, rank_ref[1] % 8
    place_blocks(last_ref, ((4, 0), (4, 1)), core, z, right_ref, columns_ref)
    place_blocks(blocks_ref, SIDE, 1 - core, z, right_ref, columns_ref)


def build_kernel(right_ref, columns_ref, mass_ref, left_ref, kernel_ref, send_ref):
    groups, own, width = left_ref.shape
    length = groups * own
    right = right_ref.reshape(length, width)
    columns = columns_ref.reshape(length, LANES)
    left = left_ref.reshape(length, width)
    sums = []
    for tile in range(0, length, TILE):
        squares = []
        for piece in range(tile, tile + TILE, LANES):
            wide = left[piece : piece + LANES, :].astype(jnp.float32)
            squares.append(row_of_sums(wide[:, :LANES] * wide[:, :LANES] + wide[:, LANES:] * wide[:, LANES:]))
        left_squares = (-0.5 * SCALE) * jnp.concatenate(squares, axis=1)
        total = jnp.zeros((8, TILE), jnp.float32)
        for start in range(0, length, ROWS):
            rows = slice(start, start + ROWS)
            inner = lax.dot_general(
                right[rows, :], left[tile : tile + TILE, :], (((1,), (1,)), ((), ())), preferred_element_type=jnp.float32
            )
            entries = jnp.exp2((SCALE * inner + left_squares) + repeated(columns[rows, :], TILE))
            kernel_ref[rows, tile : tile + TILE] = entries
            total = total + jnp.sum(entries.reshape(ROWS // 8, 8, TILE), axis=0)
        sums.append(jnp.sum(total, axis=0, keepdims=True))
    pieces = [total[:, piece] for total in sums for piece in lane_pieces(TILE)]
    send = jnp.concatenate(pieces + [mass_ref[...]], axis=1)
    for d in range(groups):
        send_ref[d] = send


def last_rows(got_ref, length, own):
    return jnp.concatenate([got_ref[d, :, length : length + own] for d in range(got_ref.shape[0])], axis=1)


def as_rows(row):
    return jnp.concatenate([row[:, piece] for piece in lane_pieces(row.shape[1])], axis=0)


def own_piece(flat_ref, rank, own):
    start = rank * own
    row, lane = start // LANES, start % LANES
    shift = (LANES - lane) % LANES
    first = pltpu.roll(jnp.broadcast_to(flat_ref[pl.ds(row, 1), :], (8, LANES)), shift, 1)
    second = pltpu.roll(jnp.broadcast_to(flat_ref[pl.ds(row + 1, 1), :], (8, LANES)), shift, 1)
    lanes = lax.broadcasted_iota(jnp.int32, (8, LANES), 1)
    return jnp.where(lanes < LANES - lane, first, second)[0:1]


def row_sums_kernel(total, own, rank_ref, kernel_ref, got_ref, send_ref, partial, flat):
    groups = got_ref.shape[0]
    length = groups * own
    count = length // LANES
    potential = -0.5 * jnp.log(as_rows(jnp.sum(got_ref[:, :, :length], axis=0)))
    flat[:count, :] = potential
    flat[count:, :] = jnp.zeros((flat.shape[0] - count, LANES), jnp.float32)
    growth = jnp.exp(potential)
    mass = last_rows(got_ref, length, own) * (1.0 / total)
    weight = jnp.concatenate([growth[n : n + 1] * mass[:, piece] for n, piece in enumerate(lane_pieces(length))], axis=1)

    def step(n, carry):
        rows = pl.ds(pl.multiple_of(n * 512, 512), 512)
        weighted = kernel_ref[rows, :] * weight
        partial[rows, :] = sum(weighted[:, piece] for piece in lane_pieces(length))
        return carry

    lax.fori_loop(0, length // 512, step, 0)
    own_mass = got_ref[rank_ref[0], :, length:] * (1.0 / total)
    mine = own_piece(flat, rank_ref[0], own) + jnp.log(own_mass)
    pieces = [row_of_sums(partial[piece, :]) for piece in lane_pieces(length)]
    send = jnp.concatenate(pieces + [mine], axis=1)
    for d in range(groups):
        send_ref[d] = send


def column_sums_kernel(own, rank_ref, kernel_ref, got_ref, send_ref, mine_ref, columns, flat):
    groups = got_ref.shape[0]
    length = groups * own
    count = length // LANES
    logs = jnp.log(as_rows(jnp.sum(got_ref[:, :, :length], axis=0)))
    before = as_rows(last_rows(got_ref, length, own))
    potential = 0.5 * (before - logs)
    flat[:count, :] = potential
    flat[count:, :] = jnp.zeros((flat.shape[0] - count, LANES), jnp.float32)
    growth = jnp.exp(potential)
    store_columns([growth[n : n + 1] for n in range(count)], columns)

    def step(n, sums):
        rows = pl.ds(pl.multiple_of(n * 16, 16), 16)
        weighted = kernel_ref[rows, :] * repeated(columns[rows, :], length)
        return sums + (weighted[:8] + weighted[8:])

    sums = lax.fori_loop(0, length // 16, step, jnp.zeros((8, length), jnp.float32), unroll=8)
    sums = jnp.sum(sums, axis=0, keepdims=True)
    for d in range(groups):
        send_ref[d] = jnp.concatenate([sums[:, d * own : (d + 1) * own], jnp.zeros((1, LANES - own), jnp.float32)], axis=1)
    mine_ref[...] = own_piece(flat, rank_ref[1], own)[:, :own]


def shards(points, mass):
    own, width = points.shape
    groups = 16
    length = groups * own
    total = length * groups
    f32 = jnp.float32
    ranks = jnp.stack([lax.axis_index(ROW), lax.axis_index(COL)]).astype(jnp.int32)
    block = pl.pallas_call(
        functools.partial(block_kernel, total),
        out_shape=jax.ShapeDtypeStruct((2 * own + EXTRA, LANES), points.dtype),
        in_specs=[HBM, HBM],
        out_specs=VMEM,
        scratch_shapes=[
            pltpu.VMEM((own, width), points.dtype),
            pltpu.VMEM((1, own), f32),
            pltpu.SemaphoreType.DMA((2,)),
        ],
        compiler_params=PARAMS,
    )(*(pltpu.with_memory_space_constraint(a, pltpu.HBM) for a in (points, mass.reshape(1, own))))
    send = pl.pallas_call(
        copies_kernel,
        out_shape=jax.ShapeDtypeStruct((groups, own, width), points.dtype),
        in_specs=[VMEM],
        out_specs=HBM,
        scratch_shapes=[pltpu.VMEM((own, width), points.dtype), pltpu.SemaphoreType.DMA((groups,))],
        compiler_params=PARAMS,
    )(block)
    swap = [(0, 1), (1, 0)]
    other, send = lax.optimization_barrier((lax.ppermute(block, "k", swap), send))
    pair = jnp.stack([block, other])
    first = along_z(pair, 2)
    last, second = along_z(first, 2), along_z(jnp.concatenate([pair, first]), 1)
    last, second = lax.optimization_barrier((last, second))
    side = jnp.concatenate([first, second])
    far = lax.ppermute(side, "k", swap)
    left = lax.all_to_all(send, ROW, 0, 0)
    ordered = [
        jax.ShapeDtypeStruct((groups, own, width), points.dtype),
        jax.ShapeDtypeStruct((groups, own, LANES), f32),
    ]
    right, columns, own_mass = pl.pallas_call(
        near_kernel,
        out_shape=ordered + [jax.ShapeDtypeStruct((1, LANES), f32)],
        in_specs=[SMEM, VMEM, VMEM],
        out_specs=[VMEM, VMEM, VMEM],
        compiler_params=PARAMS,
    )(ranks, pair, side)
    right, columns = pl.pallas_call(
        far_kernel,
        out_shape=ordered,
        in_specs=[SMEM] + [VMEM] * 4,
        out_specs=[VMEM, VMEM],
        input_output_aliases={3: 0, 4: 1},
        compiler_params=PARAMS,
    )(ranks, far, last, right, columns)
    message = jax.ShapeDtypeStruct((groups, 1, length + LANES), f32)
    kernel, send = pl.pallas_call(
        build_kernel,
        out_shape=[jax.ShapeDtypeStruct((length, length), f32), message],
        in_specs=[VMEM] * 4,
        out_specs=[VMEM, VMEM],
        compiler_params=PARAMS,
    )(right, columns, own_mass, left)
    got = lax.all_to_all(send, ROW, 0, 0)
    send = pl.pallas_call(
        functools.partial(row_sums_kernel, total, own),
        out_shape=message,
        in_specs=[SMEM, VMEM, VMEM],
        out_specs=VMEM,
        scratch_shapes=[pltpu.VMEM((length, LANES), f32), pltpu.VMEM((16, LANES), f32)],
        compiler_params=PARAMS,
    )(ranks, kernel, got)
    got = lax.all_to_all(send, COL, 0, 0)
    send, mine = pl.pallas_call(
        functools.partial(column_sums_kernel, own),
        out_shape=[jax.ShapeDtypeStruct((groups, 1, LANES), f32), jax.ShapeDtypeStruct((1, own), f32)],
        in_specs=[SMEM, VMEM, VMEM],
        out_specs=[VMEM, VMEM],
        scratch_shapes=[pltpu.VMEM((length, LANES), f32), pltpu.VMEM((16, LANES), f32)],
        compiler_params=PARAMS,
    )(ranks, kernel, got)
    sums = jnp.sum(lax.all_to_all(send, ROW, 0, 0), axis=0)[:, :own]
    return (0.5 * (mine - jnp.log(sums))).reshape(own)


def solution(mesh):
    fine = Mesh(mesh.devices.reshape(4, 2, 2, 2, 8), AXES)
    return jax.shard_map(
        shards,
        mesh=fine,
        in_specs=(P(AXES, None), P(AXES)),
        out_specs=P(AXES),
        check_vma=False,
    )
```
